32 devices in a mesh: section: 2 (over core), blk: 8 (over z, y), head: 2 (over x).
Axes of the slice: x: 2, y: 2, z: 4, core: 2. Of those that a mesh axis runs over, the one named last changes fastest.
Arguments:
- queries: bfloat16 [2, 2048, 8192], P('section', ('blk', 'head')), may hold values from -96 to 96
- key_vectors: bfloat16 [2, 2048, 1024], P('section', ('blk', 'head')), may hold values from -6 to 6
- value_vectors: bfloat16 [2, 2048, 1024], P('section', ('blk', 'head')), may hold values from -6 to 6
- residual: bfloat16 [2048, 8192], P('blk', 'head'), may hold values from -128 to 128
- pair_order: int32 [8], replicated, may hold values from 0 to 7, as said below
- probe_gain: float32 [2, 8192], P('section', 'head'), may hold values from 0.1 to 1.9
- probe_weight: float32 [2, 8192], P('section', 'head'), may hold values from -0.0625 to 0.0625
Outputs:
- hidden_out: bfloat16 [2, 2048, 8192], P('section', 'blk', 'head')
- rewards: float32 [2, 2048], P('section', 'blk')
The draws below stay inside these ranges and needn't reach their ends.
Inputs may be any that keep to these rules, and one draw needn't show every extreme that they name: `pair_order`: each value appears once.
All inputs are finite; a program needn't handle non-finite values.
Results may differ from the reference program's by a relative error of at most 0.004.
Values may be sent and summed in bfloat16 or wider, within the bound.
A program may use at most 64 MiB of HBM per device.

```python
import jax
import jax.numpy as jnp
from jax import lax

D = 8192
HEADS = 64
KV_HEADS = 8
HEAD_DIM = 128
TOK_BLK = 256
TOKENS = 2048
LAYERS = 2
N_BLK = 8


def block_order(key):
    return jax.random.permutation(jax.random.fold_in(key, 11), N_BLK).astype(jnp.int32)


def draw_pair_order(key, part):
    return block_order(key)


def draw_key_vectors(key, part):
    base = jax.random.normal(jax.random.fold_in(key, 31), (LAYERS, TOKENS, KV_HEADS * HEAD_DIM), jnp.float32)
    base = jnp.clip(base, -6.0, 6.0)
    return base.astype(jnp.bfloat16)


def draw_queries(key, part):
    base = jax.random.normal(jax.random.fold_in(key, 33), (LAYERS, TOKENS, D), jnp.float32)
    base = jnp.clip(base, -6.0, 6.0)
    return base.astype(jnp.bfloat16)


def draw_residual(key, part):
    noise = jax.random.normal(jax.random.fold_in(key, 41), (TOKENS, D), jnp.float32)
    noise = jnp.clip(noise, -6.0, 6.0)
    columns = jnp.arange(D, dtype=jnp.float32) / D
    result = noise * jnp.power(3.0, 0.5 * columns)[None, :]
    return jnp.clip(result, -128.0, 128.0).astype(jnp.bfloat16)


def block_scale(key, shape, shards, low, top_value):
    factor_of = 1.0
    for dim, shards_of in shards:
        heights = jax.random.uniform(jax.random.fold_in(jax.random.fold_in(key, 6), dim), (shards_of,), jnp.float32, low / len(shards), top_value / len(shards))
        factor_of = factor_of * jnp.repeat(jnp.exp(heights), shape[dim] // shards_of).reshape((-1,) + (1,) * (len(shape) - 1 - dim))
    return factor_of


def centred(stream_key, shape, width, bound, shards=(), held_as=jnp.bfloat16):
    drawn = width * jax.random.normal(stream_key, shape, jnp.float32)
    if shards:
        drawn = drawn * block_scale(stream_key, shape, shards, -0.22, 0.18)
    return jnp.clip(drawn, -bound, bound).astype(held_as)


def setup_inputs(seed: int = 0) -> dict:
    streams_of = jax.random.split(jax.random.key(seed), 8)
    return {
        "queries": draw_queries(jax.random.fold_in(streams_of[7], 71), 0),
        "key_vectors": draw_key_vectors(jax.random.fold_in(streams_of[7], 71), 0),
        "value_vectors": centred(streams_of[2], (LAYERS, TOKENS, KV_HEADS * HEAD_DIM), 1.0, 6.0, ((0, 2), (1, 16))),
        "residual": draw_residual(jax.random.fold_in(streams_of[7], 71), 0),
        "pair_order": draw_pair_order(jax.random.fold_in(streams_of[7], 71), 0),
        "probe_gain": jnp.clip(1.0 + 0.18 * jax.random.normal(streams_of[5], (LAYERS, D), jnp.float32), 0.1, 1.9),
        "probe_weight": centred(streams_of[6], (LAYERS, D), D ** -0.5, 0.0625, ((0, 2), (1, 2)), jnp.float32),
    }


def token_positions(pair_order):
    span_rows = TOK_BLK // 2
    row_index = jnp.arange(TOKENS, dtype=jnp.int32)
    shard = row_index // TOK_BLK
    within = row_index % TOK_BLK
    lower = pair_order[shard].astype(jnp.int32)
    which = jnp.where(within < span_rows, lower, 2 * N_BLK - 1 - lower)
    return (which * span_rows + within % span_rows).astype(jnp.int32)

def attention(queries, key_vectors, value_vectors, positions):
    group = HEADS // KV_HEADS
    factor = HEAD_DIM ** (-0.5)
    causal = positions[None, :] <= positions[:, None]

    def one_head(head):
        q_head = lax.dynamic_slice_in_dim(queries, head * HEAD_DIM, HEAD_DIM, 1)
        offset = head // group * HEAD_DIM
        k_head = lax.dynamic_slice_in_dim(key_vectors, offset, HEAD_DIM, 1)
        v_head = lax.dynamic_slice_in_dim(value_vectors, offset, HEAD_DIM, 1)
        scores = jnp.dot(q_head, k_head.T, preferred_element_type=jnp.float32) * factor
        scores = jnp.where(causal, scores, -jnp.inf)
        largest = lax.optimization_barrier(jnp.max(scores, axis=1, keepdims=True))
        weights = jnp.exp(scores - largest)
        totals = lax.optimization_barrier(jnp.sum(weights, axis=1, keepdims=True))
        mixed = jnp.dot(weights.astype(jnp.bfloat16), v_head, preferred_element_type=jnp.float32)
        return mixed / totals
    stacked = lax.map(one_head, jnp.arange(HEADS, dtype=jnp.int32))
    return jnp.transpose(stacked, (1, 0, 2)).reshape(TOKENS, D)

def reference(queries, key_vectors, value_vectors, residual, pair_order, probe_gain, probe_weight):
    positions = token_positions(pair_order)
    stream = residual
    hidden = []
    rewards = []
    for layer in range(LAYERS):
        attended = attention(queries[layer], key_vectors[layer], value_vectors[layer], positions)
        stream = (stream.astype(jnp.float32) + attended).astype(jnp.bfloat16)
        widened = stream.astype(jnp.float32)
        squares = lax.optimization_barrier(jnp.mean(widened * widened, axis=-1))
        products = lax.optimization_barrier(jnp.sum(widened * probe_gain[layer] * probe_weight[layer], axis=-1))
        rewards.append(products * lax.rsqrt(squares + 1e-05))
        hidden.append(stream)
    return (jnp.stack(hidden), jnp.stack(rewards))
```

```python
import functools
import math

import jax
import jax.numpy as jnp
from jax import lax
from jax.experimental import pallas as pl
from jax.experimental.pallas import tpu as pltpu
from jax.sharding import PartitionSpec as P

HEAD_DIM = 128
LOW = -1e30
MESH = pl.DeviceIdType.MESH


def kernel(
    sizes,
    order_ref,
    q_ref,
    k_ref,
    v_ref,
    res_ref,
    gain_ref,
    weight_ref,
    out_ref,
    reward_ref,
    kvbufs,
    qbufs,
    base,
    accs,
    maxima,
    totals,
    squares,
    products,
    parts,
    local_sem,
    xkv_send,
    xkv_recv,
    xq_send,
    xq_recv,
    ring_send,
    ring_recv,
    hand_send,
    hand_recv,
    part_send,
    part_recv,
):
    n, heads, kvl, group, span, rows, dirs = sizes
    phases = kvl // dirs
    steps = n + 1
    width = group * HEAD_DIM
    per_half = heads // 2
    sec = lax.axis_index("section")
    me = lax.axis_index("blk")
    h = lax.axis_index("head")

    def index_of(place):
        return jnp.where(2 * place < n, 2 * place, 2 * (n - 1 - place) + 1)

    place = jnp.where(me % 2 == 0, me // 2, n - 1 - me // 2)
    right = index_of((place + 1) % n)
    left = index_of((place + n - 1) % n)

    barrier = pltpu.get_barrier_semaphore()
    for to in (left, right):
        pl.semaphore_signal(barrier, inc=1, device_id={"blk": to}, device_id_type=MESH)
    for k in range(1, heads):
        pl.semaphore_signal(barrier, inc=1, device_id={"head": (h + k) % heads}, device_id_type=MESH)
    pl.semaphore_signal(barrier, inc=1, device_id={"section": 1 - sec}, device_id_type=MESH)
    pl.semaphore_wait(barrier, heads + 2)

    def rows_of(source):
        return source // per_half, pl.ds(pl.multiple_of((source % per_half) * rows, rows), rows)

    half_own, at_own = rows_of(h)

    def local_kv(j):
        cols = pl.ds(pl.multiple_of((h * kvl + j) * HEAD_DIM, HEAD_DIM), HEAD_DIM)
        return [
            pltpu.make_async_copy(
                ref.at[:, cols],
                kvbufs[j // dirs].at[j % dirs, me, half_own, at_own, pl.ds(i * HEAD_DIM, HEAD_DIM)],
                local_sem.at[i, j],
            )
            for i, ref in enumerate((k_ref, v_ref))
        ]

    def local_q(j):
        cols = pl.ds(pl.multiple_of((h * kvl + j) * width, width), width)
        return pltpu.make_async_copy(
            q_ref.at[:, cols], qbufs[j // dirs].at[j % dirs, half_own, at_own, :], local_sem.at[2, j]
        )

    def local_base():
        return pltpu.make_async_copy(res_ref, base, local_sem.at[3, 0])

    def cross_kv(j, k):
        to = (h + k) % heads
        cols = pl.ds(pl.multiple_of((to * kvl + j) * HEAD_DIM, HEAD_DIM), HEAD_DIM)
        return [
            pltpu.make_async_remote_copy(
                src_ref=ref.at[:, cols],
                dst_ref=kvbufs[j // dirs].at[j % dirs, me, half_own, at_own, pl.ds(i * HEAD_DIM, HEAD_DIM)],
                send_sem=xkv_send.at[i, j, k],
                recv_sem=xkv_recv.at[i, j, k],
                device_id={"head": to},
                device_id_type=MESH,
            )
            for i, ref in enumerate((k_ref, v_ref))
        ]

    def cross_kv_arrived(j, k):
        half, at = rows_of((h + heads - k) % heads)
        for i in range(2):
            piece = kvbufs[j // dirs].at[j % dirs, me, half, at, pl.ds(i * HEAD_DIM, HEAD_DIM)]
            pltpu.make_async_copy(piece, piece, xkv_recv.at[i, j, k]).wait()

    def cross_q(j, k):
        to = (h + k) % heads
        cols = pl.ds(pl.multiple_of((to * kvl + j) * width, width), width)
        return pltpu.make_async_remote_copy(
            src_ref=q_ref.at[:, cols],
            dst_ref=qbufs[j // dirs].at[j % dirs, half_own, at_own, :],
            send_sem=xq_send.at[j, k],
            recv_sem=xq_recv.at[j, k],
            device_id={"head": to},
            device_id_type=MESH,
        )

    def queries_here(j):
        local_q(j).wait()
        for k in range(1, heads):
            half, at = rows_of((h + heads - k) % heads)
            piece = qbufs[j // dirs].at[j % dirs, half, at, :]
            pltpu.make_async_copy(piece, piece, xq_recv.at[j, k]).wait()

    def hop(d, ph, s, r):
        away = (place + n - s) % n if d == 0 else (place + s) % n
        half, at = rows_of(r)
        piece = kvbufs[ph].at[d, index_of(away), half, at, :]
        return pltpu.make_async_remote_copy(
            src_ref=piece,
            dst_ref=piece,
            send_sem=ring_send.at[d, ph, s, r],
            recv_sem=ring_recv.at[d, ph, s, r],
            device_id={"blk": right if d == 0 else left},
            device_id_type=MESH,
        )

    def hop_arrived(d, ph, s, r):
        away = (place + n - s) % n if d == 0 else (place + s) % n
        half, at = rows_of(r)
        piece = kvbufs[ph].at[d, index_of(away), half, at, :]
        pltpu.make_async_copy(piece, piece, ring_recv.at[d, ph, s - 1, r]).wait()

    def first_hops(ph):
        for d in range(dirs):
            for copy in local_kv(ph * dirs + d):
                copy.wait()
            hop(d, ph, 0, h).start()
        for k in range(1, heads):
            for d in range(dirs):
                cross_kv_arrived(ph * dirs + d, k)
                hop(d, ph, 0, (h + heads - k) % heads).start()

    def service(ph, s):
        for r in range(heads):
            for d in range(dirs):
                hop_arrived(d, ph, s, r)

                @pl.when(s < n - 1)
                def _():
                    hop(d, ph, s, r).start()

    for j in range(kvl):
        for k in range(1, heads):
            for copy in cross_kv(j, k):
                copy.start()
    for j in range(kvl):
        for copy in local_kv(j):
            copy.start()
    for j in range(kvl):
        for k in range(1, heads):
            cross_q(j, k).start()
    for j in range(kvl):
        local_q(j).start()

    @pl.when(sec == 0)
    def _():
        local_base().start()

    maxima[...] = jnp.full_like(maxima, LOW)
    totals[...] = jnp.zeros_like(totals)
    squares[...] = jnp.zeros_like(squares)
    products[...] = jnp.zeros_like(products)
    accs[n // 2] = jnp.zeros_like(accs[n // 2])

    lower = jnp.int32(0)
    for b in range(n):
        lower = jnp.where(me == b, order_ref[b], lower)
    lower_steps = (lower + 2) // 2
    scale = math.log2(math.e) / math.sqrt(HEAD_DIM)
    pairs = max(1, group // 2)
    lanes = width // pairs

    def where_is(c):
        first = jnp.minimum(c, 2 * n - 1 - c)
        b = jnp.int32(0)
        for i in range(n):
            b = jnp.where(order_ref[i] == first, i, b)
        return b, jnp.where(c < n, 0, 1)

    def chunk(ph, d, t):
        in_lower = t < lower_steps
        half = jnp.where(in_lower, 0, 1)
        own = jnp.where(in_lower, lower, 2 * n - 1 - lower)
        key = jnp.where(in_lower, t, t - lower_steps)
        fresh = jnp.logical_or(t == 0, t == lower_steps)
        b0, h0 = where_is(2 * key)
        b1, h1 = where_is(2 * key + 1)
        kv0 = kvbufs[ph][d, b0, h0]
        kv1 = kvbufs[ph][d, b1, h1]
        keys = jnp.concatenate([kv0[:, :HEAD_DIM], kv1[:, :HEAD_DIM]], axis=0)
        values = jnp.concatenate([kv0[:, HEAD_DIM:], kv1[:, HEAD_DIM:]], axis=0)
        limit = (own - 2 * key) * span
        ahead = lax.broadcasted_iota(jnp.int32, (2 * span, lanes), 0) - lax.rem(
            lax.broadcasted_iota(jnp.int32, (2 * span, lanes), 1), span
        )
        seen = ahead <= limit
        before = jnp.where(t == 0, n // 2, jnp.minimum(t - 1, n // 2))
        now = jnp.minimum(t, n // 2)
        old_max = jnp.where(fresh, LOW, maxima[before])
        old_total = totals[before]
        for p in range(pairs):
            at = slice(p * lanes, (p + 1) * lanes)
            q = qbufs[ph][d, half, :, p * lanes : (p + 1) * lanes]
            q = jnp.concatenate(
                [q[:, i * HEAD_DIM : (i + 1) * HEAD_DIM] for i in range(lanes // HEAD_DIM)], axis=0
            )
            scores = lax.dot_general(
                keys, q, (((1,), (1,)), ((), ())), preferred_element_type=jnp.float32
            )
            scores = jnp.where(seen, scores, LOW)
            new_max = jnp.maximum(old_max[:, at], jnp.max(scores, axis=0, keepdims=True))
            weights = jnp.exp2((scores - new_max) * scale)
            fade = jnp.exp2((old_max[:, at] - new_max) * scale)
            total = old_total[:, at] * fade + jnp.sum(weights, axis=0, keepdims=True)
            mixed = lax.dot_general(
                values,
                weights.astype(jnp.bfloat16),
                (((0,), (0,)), ((), ())),
                preferred_element_type=jnp.float32,
            )
            accs[now, :, at] = accs[before, :, at] * fade + mixed
            maxima[now, :, at] = new_max
            totals[now, :, at] = total

    def hand(j):
        piece = base.at[:, pl.ds(pl.multiple_of(j * width, width), width)]
        return pltpu.make_async_remote_copy(
            src_ref=out_ref.at[:, pl.ds(pl.multiple_of(j * width, width), width)],
            dst_ref=piece,
            send_sem=hand_send.at[j],
            recv_sem=hand_recv.at[j],
            device_id={"section": 1 - sec},
            device_id_type=MESH,
        )

    def finish(j):
        @pl.when(jnp.logical_and(sec == 0, j == 0))
        def _():
            local_base().wait()

        @pl.when(sec == 1)
        def _():
            hand(j).wait_recv()

        for half in range(2):
            slot = lower_steps - 1 if half == 0 else n // 2
            inverse = 1.0 / totals[slot]
            for g in range(group):
                at = slice(g * HEAD_DIM, (g + 1) * HEAD_DIM)
                cols = pl.ds(pl.multiple_of(j * width + g * HEAD_DIM, HEAD_DIM), HEAD_DIM)
                r = slice(half * span, (half + 1) * span)
                attended = (accs[slot, :, at] * inverse[:, at]).T
                stream = (base[r, cols].astype(jnp.float32) + attended).astype(jnp.bfloat16)
                out_ref[r, cols] = stream
                wide = stream.astype(jnp.float32)
                squares[half] += wide * wide
                products[half] += wide * (gain_ref[:, cols] * weight_ref[:, cols])

        @pl.when(sec == 0)
        def _():
            hand(j).start()

    def task(ph, g):
        d = g // steps
        t = g % steps

        @pl.when(g == 0)
        def _():
            for i in range(dirs):
                queries_here(ph * dirs + i)

        chunk(ph, d, t)

        @pl.when(t == steps - 1)
        def _():
            finish(ph * dirs + d)

    work = dirs * steps
    first_hops(0)
    for ph in range(phases):
        each = 0 if ph == 0 else -(-work // (n - 1))

        def step(s, carry, ph=ph, each=each):
            service(ph, s)
            if ph + 1 < phases:

                @pl.when(s == 1)
                def _():
                    first_hops(ph + 1)

            if each:

                def one(g, c):
                    task(ph - 1, g)
                    return c

                lax.fori_loop((s - 1) * each, jnp.minimum(s * each, work), one, 0)
            return carry

        lax.fori_loop(1, n, step, 0)

    def last(g, c):
        task(phases - 1, g)
        return c

    lax.fori_loop(0, work, last, 0)

    def totals_of(ref):
        return [jnp.sum(ref[half].T, axis=0, keepdims=True) for half in range(2)]

    parts[h] = jnp.concatenate(totals_of(squares) + totals_of(products), axis=0)

    def share(k):
        return pltpu.make_async_remote_copy(
            src_ref=parts.at[h],
            dst_ref=parts.at[h],
            send_sem=part_send.at[k],
            recv_sem=part_recv.at[k],
            device_id={"head": (h + k) % heads},
            device_id_type=MESH,
        )

    for k in range(1, heads):
        share(k).start()
    for k in range(1, heads):
        piece = parts.at[(h + heads - k) % heads]
        pltpu.make_async_copy(piece, piece, part_recv.at[k]).wait()
    both = parts[0]
    for k in range(1, heads):
        both = both + parts[k]
    features = heads * kvl * width
    reward_ref[...] = both[2:4] * lax.rsqrt(both[0:2] / features + 1e-05)

    for k in range(1, heads):
        share(k).wait_send()
        for j in range(kvl):
            for copy in cross_kv(j, k):
                copy.wait_send()
            cross_q(j, k).wait_send()
    for ph in range(phases):

        def sent(s, carry, ph=ph):
            for r in range(heads):
                for d in range(dirs):
                    hop(d, ph, s, r).wait_send()
            return carry

        lax.fori_loop(0, n - 1, sent, 0)

    @pl.when(sec == 0)
    def _():
        for j in range(kvl):
            hand(j).wait_send()


def body(queries, key_vectors, value_vectors, residual, pair_order, probe_gain, probe_weight):
    n = lax.axis_size("blk")
    heads = lax.axis_size("head")
    rows, features = queries.shape[1:]
    kvl = key_vectors.shape[2] // HEAD_DIM // heads
    group = features // key_vectors.shape[2]
    span = residual.shape[0] // 2
    dirs = 2 if kvl % 2 == 0 else 1
    phases = kvl // dirs
    width = group * HEAD_DIM
    local = residual.shape[1]
    sizes = (n, heads, kvl, group, span, rows, dirs)
    dma = pltpu.SemaphoreType.DMA
    anywhere = pl.BlockSpec(memory_space=pl.ANY)
    vmem = pl.BlockSpec(memory_space=pltpu.VMEM)
    slots = n // 2 + 1
    stream, reward = pl.pallas_call(
        functools.partial(kernel, sizes),
        out_shape=(
            jax.ShapeDtypeStruct((2 * span, local), jnp.bfloat16),
            jax.ShapeDtypeStruct((2, span), jnp.float32),
        ),
        in_specs=[pl.BlockSpec(memory_space=pltpu.SMEM)] + [anywhere] * 4 + [vmem] * 2,
        out_specs=(vmem, vmem),
        scratch_shapes=[
            [pltpu.VMEM((dirs, n, 2, span, 2 * HEAD_DIM), jnp.bfloat16)] * phases,
            [pltpu.VMEM((dirs, 2, span, width), jnp.bfloat16)] * phases,
            pltpu.VMEM((2 * span, local), jnp.bfloat16),
            pltpu.VMEM((slots, HEAD_DIM, width), jnp.float32),
            pltpu.VMEM((slots, 1, width), jnp.float32),
            pltpu.VMEM((slots, 1, width), jnp.float32),
            pltpu.VMEM((2, span, HEAD_DIM), jnp.float32),
            pltpu.VMEM((2, span, HEAD_DIM), jnp.float32),
            pltpu.VMEM((heads, 4, span), jnp.float32),
            dma((4, kvl)),
            dma((2, kvl, heads)),
            dma((2, kvl, heads)),
            dma((kvl, heads)),
            dma((kvl, heads)),
            dma((dirs, phases, n, heads)),
            dma((dirs, phases, n, heads)),
            dma((kvl,)),
            dma((kvl,)),
            dma((heads,)),
            dma((heads,)),
        ],
        compiler_params=pltpu.CompilerParams(
            collective_id=0, has_side_effects=True, vmem_limit_bytes=48 * 1024 * 1024
        ),
        name="attention",
    )(pair_order, queries[0], key_vectors[0], value_vectors[0], residual, probe_gain, probe_weight)
    return stream[None], reward.reshape(1, 2 * span)


def solution(mesh):
    return jax.shard_map(
        body,
        mesh=mesh,
        in_specs=(
            P("section", ("blk", "head"), None),
            P("section", ("blk", "head"), None),
            P("section", ("blk", "head"), None),
            P("blk", "head"),
            P(),
            P("section", "head"),
            P("section", "head"),
        ),
        out_specs=(P("section", "blk", "head"), P("section", "blk")),
        check_vma=False,
    )
```

```python
import functools
import math

import jax
import jax.numpy as jnp
from jax import lax
from jax.experimental import pallas as pl
from jax.experimental.pallas import tpu as pltpu
from jax.sharding import PartitionSpec as P

HEAD_DIM = 128
LOW = -1e30
MESH = pl.DeviceIdType.MESH


def kernel(
    sizes,
    order_ref,
    q_ref,
    k_ref,
    v_ref,
    res_ref,
    gain_hbm,
    weight_hbm,
    out_ref,
    reward_ref,
    kvbufs,
    qbufs,
    turned,
    base,
    gain_ref,
    weight_ref,
    accs,
    maxima,
    totals,
    squares,
    products,
    parts,
    local_sem,
    base_sem,
    xkv_send,
    xkv_recv,
    xq_send,
    xq_recv,
    ring_send,
    ring_recv,
    hand_send,
    hand_recv,
    part_send,
    part_recv,
):
    n, heads, kvl, group, span, rows = sizes
    steps = n + 1
    width = group * HEAD_DIM
    per_half = heads // 2
    sec = lax.axis_index("section")
    me = lax.axis_index("blk")
    h = lax.axis_index("head")

    def index_of(place):
        return jnp.where(2 * place < n, 2 * place, 2 * (n - 1 - place) + 1)

    place = jnp.where(me % 2 == 0, me // 2, n - 1 - me // 2)
    right = index_of((place + 1) % n)
    left = index_of((place + n - 1) % n)

    barrier = pltpu.get_barrier_semaphore()
    for to in (left, right):
        pl.semaphore_signal(barrier, inc=1, device_id={"blk": to}, device_id_type=MESH)
    for k in range(1, heads):
        pl.semaphore_signal(barrier, inc=1, device_id={"head": (h + k) % heads}, device_id_type=MESH)
    pl.semaphore_signal(barrier, inc=1, device_id={"section": 1 - sec}, device_id_type=MESH)
    pl.semaphore_wait(barrier, heads + 2)

    def rows_of(source):
        return source // per_half, pl.ds(pl.multiple_of((source % per_half) * rows, rows), rows)

    half_own, at_own = rows_of(h)

    def local_kv(j):
        cols = pl.ds(pl.multiple_of((h * kvl + j) * HEAD_DIM, HEAD_DIM), HEAD_DIM)
        return [
            pltpu.make_async_copy(
                ref.at[:, cols],
                kvbufs[j].at[me, half_own, at_own, pl.ds(i * HEAD_DIM, HEAD_DIM)],
                local_sem.at[i, j],
            )
            for i, ref in enumerate((k_ref, v_ref))
        ]

    def local_q(j):
        cols = pl.ds(pl.multiple_of((h * kvl + j) * width, width), width)
        return pltpu.make_async_copy(
            q_ref.at[:, cols], qbufs[j].at[half_own, at_own, :], local_sem.at[2, j]
        )

    def local_base():
        return pltpu.make_async_copy(res_ref, base, base_sem.at[0])

    def local_probe():
        return [
            pltpu.make_async_copy(gain_hbm, gain_ref, base_sem.at[1]),
            pltpu.make_async_copy(weight_hbm, weight_ref, base_sem.at[2]),
        ]

    def cross_kv(j, k):
        to = (h + k) % heads
        cols = pl.ds(pl.multiple_of((to * kvl + j) * HEAD_DIM, HEAD_DIM), HEAD_DIM)
        return [
            pltpu.make_async_remote_copy(
                src_ref=ref.at[:, cols],
                dst_ref=kvbufs[j].at[me, half_own, at_own, pl.ds(i * HEAD_DIM, HEAD_DIM)],
                send_sem=xkv_send.at[i, j, k],
                recv_sem=xkv_recv.at[i, j, k],
                device_id={"head": to},
                device_id_type=MESH,
            )
            for i, ref in enumerate((k_ref, v_ref))
        ]

    def cross_kv_arrived(j, k):
        half, at = rows_of((h + heads - k) % heads)
        for i in range(2):
            piece = kvbufs[j].at[me, half, at, pl.ds(i * HEAD_DIM, HEAD_DIM)]
            pltpu.make_async_copy(piece, piece, xkv_recv.at[i, j, k]).wait()

    def cross_q(j, k):
        to = (h + k) % heads
        cols = pl.ds(pl.multiple_of((to * kvl + j) * width, width), width)
        return pltpu.make_async_remote_copy(
            src_ref=q_ref.at[:, cols],
            dst_ref=qbufs[j].at[half_own, at_own, :],
            send_sem=xq_send.at[j, k],
            recv_sem=xq_recv.at[j, k],
            device_id={"head": to},
            device_id_type=MESH,
        )

    def queries_here(j):
        local_q(j).wait()
        for k in range(1, heads):
            half, at = rows_of((h + heads - k) % heads)
            piece = qbufs[j].at[half, at, :]
            pltpu.make_async_copy(piece, piece, xq_recv.at[j, k]).wait()

    def piece_of(j, s, r, d):
        away = (place + n - s) % n if d == 0 else (place + s) % n
        half, at = rows_of(r)
        return kvbufs[j].at[index_of(away), half, at, :]

    def hop(j, s, r, d):
        piece = piece_of(j, s, r, d)
        return pltpu.make_async_remote_copy(
            src_ref=piece,
            dst_ref=piece,
            send_sem=ring_send.at[j, s, r],
            recv_sem=ring_recv.at[j, s, r],
            device_id={"blk": right if d == 0 else left},
            device_id_type=MESH,
        )

    def hop_arrived(j, s, r, d):
        piece = piece_of(j, s, r, d)
        pltpu.make_async_copy(piece, piece, ring_recv.at[j, s - 1, r]).wait()

    def first_hop(j, r):
        @pl.when(r < per_half)
        def _():
            hop(j, 0, r, 0).start()

        @pl.when(r >= per_half)
        def _():
            hop(j, 0, r, 1).start()

    def first_hops(j):
        for copy in local_kv(j):
            copy.wait()
        first_hop(j, h)
        for k in range(1, heads):
            cross_kv_arrived(j, k)
            first_hop(j, (h + heads - k) % heads)

    def service(j, s):
        for i in range(per_half):
            for d in range(2):
                r = d * per_half + i
                hop_arrived(j, s, r, d)

                @pl.when(s < n - 1)
                def _():
                    hop(j, s, r, d).start()

    for j in range(kvl):
        for k in range(1, heads):
            for copy in cross_kv(j, k):
                copy.start()
    for j in range(kvl):
        for copy in local_kv(j):
            copy.start()
    for j in range(kvl):
        for k in range(1, heads):
            cross_q(j, k).start()
    for j in range(kvl):
        local_q(j).start()

    @pl.when(sec == 0)
    def _():
        local_base().start()

    for copy in local_probe():
        copy.start()

    maxima[...] = jnp.full_like(maxima, LOW)
    totals[...] = jnp.zeros_like(totals)
    squares[...] = jnp.zeros_like(squares)
    products[...] = jnp.zeros_like(products)
    accs[n // 2] = jnp.zeros_like(accs[n // 2])

    lower = jnp.int32(0)
    for b in range(n):
        lower = jnp.where(me == b, order_ref[b], lower)
    lower_steps = (lower + 2) // 2
    scale = math.log2(math.e) / math.sqrt(HEAD_DIM)
    pairs = max(1, group // 2)
    lanes = group * span // pairs
    heads_in = lanes // span

    def where_is(c):
        first = jnp.minimum(c, 2 * n - 1 - c)
        b = jnp.int32(0)
        for i in range(n):
            b = jnp.where(order_ref[i] == first, i, b)
        return b, jnp.where(c < n, 0, 1)

    def turn(j):
        for half in range(2):
            for g in range(group):
                at = slice(g * HEAD_DIM, (g + 1) * HEAD_DIM)
                turned[half, :, g * span : (g + 1) * span] = qbufs[j][half, :, at].T

    def chunk(j, t):
        in_lower = t < lower_steps
        half = jnp.where(in_lower, 0, 1)
        own = jnp.where(in_lower, lower, 2 * n - 1 - lower)
        key = jnp.where(in_lower, t, t - lower_steps)
        fresh = jnp.logical_or(t == 0, t == lower_steps)
        b0, h0 = where_is(2 * key)
        b1, h1 = where_is(2 * key + 1)
        kv0 = kvbufs[j][b0, h0]
        kv1 = kvbufs[j][b1, h1]
        keys = jnp.concatenate([kv0[:, :HEAD_DIM], kv1[:, :HEAD_DIM]], axis=0)
        values = jnp.concatenate([kv0[:, HEAD_DIM:], kv1[:, HEAD_DIM:]], axis=0).T
        limit = (own - 2 * key) * span
        ahead = lax.broadcasted_iota(jnp.int32, (2 * span, span), 0) - lax.broadcasted_iota(
            jnp.int32, (2 * span, span), 1
        )
        seen = jnp.concatenate([ahead <= limit] * heads_in, axis=1)
        before = jnp.where(t == 0, n // 2, jnp.minimum(t - 1, n // 2))
        now = jnp.minimum(t, n // 2)
        old_max = jnp.where(fresh, LOW, maxima[before])
        old_total = totals[before]

        def at(p):
            return slice(p * lanes, (p + 1) * lanes)

        def scores_of(p):
            return jnp.dot(keys, turned[half, :, at(p)], preferred_element_type=jnp.float32)

        def soften(p, scores):
            scores = jnp.where(seen, scores, LOW)
            new_max = jnp.maximum(old_max[:, at(p)], jnp.max(scores, axis=0, keepdims=True))
            weights = jnp.exp2((scores - new_max) * scale)
            fade = jnp.exp2((old_max[:, at(p)] - new_max) * scale)
            total = old_total[:, at(p)] * fade + jnp.sum(weights, axis=0, keepdims=True)
            mixed = jnp.dot(
                values, weights.astype(jnp.bfloat16), preferred_element_type=jnp.float32
            )
            return new_max, total, fade, mixed

        def keep(p, results):
            new_max, total, fade, mixed = results
            accs[now, :, at(p)] = accs[before, :, at(p)] * fade + mixed
            maxima[now, :, at(p)] = new_max
            totals[now, :, at(p)] = total

        coming = scores_of(0)
        held = None
        for p in range(pairs):
            scores = coming
            if p + 1 < pairs:
                coming = scores_of(p + 1)
            results = soften(p, scores)
            if held is not None:
                keep(p - 1, held)
            held = results
        keep(pairs - 1, held)

    def hand(j):
        piece = base.at[:, pl.ds(pl.multiple_of(j * width, width), width)]
        return pltpu.make_async_remote_copy(
            src_ref=out_ref.at[0, :, pl.ds(pl.multiple_of(j * width, width), width)],
            dst_ref=piece,
            send_sem=hand_send.at[j],
            recv_sem=hand_recv.at[j],
            device_id={"section": 1 - sec},
            device_id_type=MESH,
        )

    def finish(j):
        if j == 0:

            @pl.when(sec == 0)
            def _():
                local_base().wait()

            for copy in local_probe():
                copy.wait()

        @pl.when(sec == 1)
        def _():
            hand(j).wait_recv()

        for half in range(2):
            slot = lower_steps - 1 if half == 0 else n // 2
            inverse = 1.0 / totals[slot]
            for g in range(group):
                at = slice(g * span, (g + 1) * span)
                cols = pl.ds(pl.multiple_of(j * width + g * HEAD_DIM, HEAD_DIM), HEAD_DIM)
                r = slice(half * span, (half + 1) * span)
                attended = (accs[slot, :, at] * inverse[:, at]).T
                stream = (base[r, cols].astype(jnp.float32) + attended).astype(jnp.bfloat16)
                out_ref[0, r, cols] = stream
                wide = stream.astype(jnp.float32)
                squares[half] += wide * wide
                products[half] += wide * (gain_ref[:, cols] * weight_ref[:, cols])

        @pl.when(sec == 0)
        def _():
            hand(j).start()

    stagger = max(1, (n - 1) // 2)
    first_hops(0)

    def slot(time, carry):
        for j in range(kvl):
            s = time - j * stagger

            @pl.when(jnp.logical_and(s >= 1, s < n))
            def _():
                service(j, s)

            if j:

                @pl.when(s == 0)
                def _():
                    first_hops(j)

        return carry

    lax.fori_loop(1, n, slot, 0)
    each = -(-steps // stagger)
    for j in range(kvl):
        queries_here(j)
        turn(j)
        if j + 1 < kvl:

            def both(i, carry, j=j):
                def one(t, c):
                    chunk(j, t)
                    return c

                lax.fori_loop(i * each, jnp.minimum((i + 1) * each, steps), one, 0)
                return slot(n + j * stagger + i, carry)

            lax.fori_loop(0, stagger, both, 0)
        else:

            def one(t, c, j=j):
                chunk(j, t)
                return c

            lax.fori_loop(0, steps, one, 0)
        finish(j)

    def totals_of(ref):
        return [jnp.sum(ref[half].T, axis=0, keepdims=True) for half in range(2)]

    parts[h] = jnp.concatenate(totals_of(squares) + totals_of(products), axis=0)

    def share(k):
        return pltpu.make_async_remote_copy(
            src_ref=parts.at[h],
            dst_ref=parts.at[h],
            send_sem=part_send.at[k],
            recv_sem=part_recv.at[k],
            device_id={"head": (h + k) % heads},
            device_id_type=MESH,
        )

    for k in range(1, heads):
        share(k).start()
    for k in range(1, heads):
        piece = parts.at[(h + heads - k) % heads]
        pltpu.make_async_copy(piece, piece, part_recv.at[k]).wait()
    both = parts[0]
    for k in range(1, heads):
        both = both + parts[k]
    features = heads * kvl * width
    reward = both[2:4] * lax.rsqrt(both[0:2] / features + 1e-05)
    reward_ref[...] = jnp.concatenate([reward[:1], reward[1:]], axis=1)

    for k in range(1, heads):
        share(k).wait_send()
        for j in range(kvl):
            for copy in cross_kv(j, k):
                copy.wait_send()
            cross_q(j, k).wait_send()
    for j in range(kvl):

        def sent(s, carry, j=j):
            for r in range(heads):
                hop(j, s, r, r // per_half).wait_send()
            return carry

        lax.fori_loop(0, n - 1, sent, 0)

    @pl.when(sec == 0)
    def _():
        for j in range(kvl):
            hand(j).wait_send()


def body(queries, key_vectors, value_vectors, residual, pair_order, probe_gain, probe_weight):
    n = lax.axis_size("blk")
    heads = lax.axis_size("head")
    rows, features = queries.shape[1:]
    kvl = key_vectors.shape[2] // HEAD_DIM // heads
    group = features // key_vectors.shape[2]
    span = residual.shape[0] // 2
    width = group * HEAD_DIM
    local = residual.shape[1]
    sizes = (n, heads, kvl, group, span, rows)
    dma = pltpu.SemaphoreType.DMA
    hbm = pl.BlockSpec(memory_space=pltpu.HBM)
    vmem = pl.BlockSpec(memory_space=pltpu.VMEM)
    slots = n // 2 + 1
    stream, reward = pl.pallas_call(
        functools.partial(kernel, sizes),
        out_shape=(
            jax.ShapeDtypeStruct((1, 2 * span, local), jnp.bfloat16),
            jax.ShapeDtypeStruct((1, 2 * span), jnp.float32),
        ),
        in_specs=[pl.BlockSpec(memory_space=pltpu.SMEM)] + [hbm] * 6,
        out_specs=(vmem, vmem),
        scratch_shapes=[
            [pltpu.VMEM((n, 2, span, 2 * HEAD_DIM), jnp.bfloat16)] * kvl,
            [pltpu.VMEM((2, span, width), jnp.bfloat16)] * kvl,
            pltpu.VMEM((2, HEAD_DIM, group * span), jnp.bfloat16),
            pltpu.VMEM((2 * span, local), jnp.bfloat16),
            pltpu.VMEM((1, local), jnp.float32),
            pltpu.VMEM((1, local), jnp.float32),
            pltpu.VMEM((slots, HEAD_DIM, group * span), jnp.float32),
            pltpu.VMEM((slots, 1, group * span), jnp.float32),
            pltpu.VMEM((slots, 1, group * span), jnp.float32),
            pltpu.VMEM((2, span, HEAD_DIM), jnp.float32),
            pltpu.VMEM((2, span, HEAD_DIM), jnp.float32),
            pltpu.VMEM((heads, 4, span), jnp.float32),
            dma((3, kvl)),
            dma((3,)),
            dma((2, kvl, heads)),
            dma((2, kvl, heads)),
            dma((kvl, heads)),
            dma((kvl, heads)),
            dma((kvl, n, heads)),
            dma((kvl, n, heads)),
            dma((kvl,)),
            dma((kvl,)),
            dma((heads,)),
            dma((heads,)),
        ],
        compiler_params=pltpu.CompilerParams(
            collective_id=0, has_side_effects=True, vmem_limit_bytes=62 * 1024 * 1024
        ),
        name="attention",
    )(pair_order, queries[0], key_vectors[0], value_vectors[0], residual, probe_gain, probe_weight)
    return stream, reward


def solution(mesh):
    return jax.shard_map(
        body,
        mesh=mesh,
        in_specs=(
            P("section", ("blk", "head"), None),
            P("section", ("blk", "head"), None),
            P("section", ("blk", "head"), None),
            P("blk", "head"),
            P(),
            P("section", "head"),
            P("section", "head"),
        ),
        out_specs=(P("section", "blk", "head"), P("section", "blk")),
        check_vma=False,
    )
```

```python
import functools
import math

import jax
import jax.numpy as jnp
from jax import lax
from jax.experimental import pallas as pl
from jax.experimental.pallas import tpu as pltpu
from jax.sharding import PartitionSpec as P

HEAD_DIM = 128
LOW = -1e30
MESH = pl.DeviceIdType.MESH


def kernel(
    sizes,
    order_ref,
    q_ref,
    k_ref,
    v_ref,
    res_ref,
    gain_hbm,
    weight_hbm,
    out_ref,
    reward_ref,
    kvbufs,
    qbufs,
    turned,
    base,
    gain_ref,
    weight_ref,
    accs,
    maxima,
    totals,
    squares,
    products,
    parts,
    local_sem,
    base_sem,
    xkv_send,
    xkv_recv,
    xq_send,
    xq_recv,
    ring_send,
    ring_recv,
    hand_send,
    hand_recv,
    part_send,
    part_recv,
):
    n, heads, kvl, group, span, rows = sizes
    steps = n + 1
    width = group * HEAD_DIM
    per_half = heads // 2
    sec = lax.axis_index("section")
    me = lax.axis_index("blk")
    h = lax.axis_index("head")

    def index_of(place):
        return jnp.where(2 * place < n, 2 * place, 2 * (n - 1 - place) + 1)

    place = jnp.where(me % 2 == 0, me // 2, n - 1 - me // 2)
    right = index_of((place + 1) % n)
    left = index_of((place + n - 1) % n)

    barrier = pltpu.get_barrier_semaphore()
    for to in (left, right):
        pl.semaphore_signal(barrier, inc=1, device_id={"blk": to}, device_id_type=MESH)
    for k in range(1, heads):
        pl.semaphore_signal(barrier, inc=1, device_id={"head": (h + k) % heads}, device_id_type=MESH)
    pl.semaphore_signal(barrier, inc=1, device_id={"section": 1 - sec}, device_id_type=MESH)
    pl.semaphore_wait(barrier, heads + 2)

    def rows_of(source):
        return source // per_half, pl.ds(pl.multiple_of((source % per_half) * rows, rows), rows)

    half_own, at_own = rows_of(h)

    def local_kv(j):
        cols = pl.ds(pl.multiple_of((h * kvl + j) * HEAD_DIM, HEAD_DIM), HEAD_DIM)
        return [
            pltpu.make_async_copy(
                ref.at[:, cols],
                kvbufs[j].at[me, half_own, at_own, pl.ds(i * HEAD_DIM, HEAD_DIM)],
                local_sem.at[i, j],
            )
            for i, ref in enumerate((k_ref, v_ref))
        ]

    def local_q(j):
        cols = pl.ds(pl.multiple_of((h * kvl + j) * width, width), width)
        return pltpu.make_async_copy(
            q_ref.at[:, cols], qbufs[j].at[half_own, at_own, :], local_sem.at[2, j]
        )

    def local_base():
        return pltpu.make_async_copy(res_ref, base, base_sem.at[0])

    def local_probe():
        return [
            pltpu.make_async_copy(gain_hbm, gain_ref, base_sem.at[1]),
            pltpu.make_async_copy(weight_hbm, weight_ref, base_sem.at[2]),
        ]

    def cross_kv(j, k):
        to = (h + k) % heads
        cols = pl.ds(pl.multiple_of((to * kvl + j) * HEAD_DIM, HEAD_DIM), HEAD_DIM)
        return [
            pltpu.make_async_remote_copy(
                src_ref=ref.at[:, cols],
                dst_ref=kvbufs[j].at[me, half_own, at_own, pl.ds(i * HEAD_DIM, HEAD_DIM)],
                send_sem=xkv_send.at[i, j, k],
                recv_sem=xkv_recv.at[i, j, k],
                device_id={"head": to},
                device_id_type=MESH,
            )
            for i, ref in enumerate((k_ref, v_ref))
        ]

    def cross_kv_arrived(j, k):
        half, at = rows_of((h + heads - k) % heads)
        for i in range(2):
            piece = kvbufs[j].at[me, half, at, pl.ds(i * HEAD_DIM, HEAD_DIM)]
            pltpu.make_async_copy(piece, piece, xkv_recv.at[i, j, k]).wait()

    def cross_q(j, k):
        to = (h + k) % heads
        cols = pl.ds(pl.multiple_of((to * kvl + j) * width, width), width)
        return pltpu.make_async_remote_copy(
            src_ref=q_ref.at[:, cols],
            dst_ref=qbufs[j].at[half_own, at_own, :],
            send_sem=xq_send.at[j, k],
            recv_sem=xq_recv.at[j, k],
            device_id={"head": to},
            device_id_type=MESH,
        )

    def queries_here(j):
        local_q(j).wait()
        for k in range(1, heads):
            half, at = rows_of((h + heads - k) % heads)
            piece = qbufs[j].at[half, at, :]
            pltpu.make_async_copy(piece, piece, xq_recv.at[j, k]).wait()

    def piece_of(j, s, r, d):
        away = (place + n - s) % n if d == 0 else (place + s) % n
        half, at = rows_of(r)
        return kvbufs[j].at[index_of(away), half, at, :]

    def hop(j, s, r, d):
        piece = piece_of(j, s, r, d)
        return pltpu.make_async_remote_copy(
            src_ref=piece,
            dst_ref=piece,
            send_sem=ring_send.at[j, s, r],
            recv_sem=ring_recv.at[j, s, r],
            device_id={"blk": right if d == 0 else left},
            device_id_type=MESH,
        )

    def hop_arrived(j, s, r, d):
        piece = piece_of(j, s, r, d)
        pltpu.make_async_copy(piece, piece, ring_recv.at[j, s - 1, r]).wait()

    def first_hop(j, r):
        @pl.when(r < per_half)
        def _():
            hop(j, 0, r, 0).start()

        @pl.when(r >= per_half)
        def _():
            hop(j, 0, r, 1).start()

    def first_hops(j):
        for copy in local_kv(j):
            copy.wait()
        first_hop(j, h)
        for k in range(1, heads):
            cross_kv_arrived(j, k)
            first_hop(j, (h + heads - k) % heads)

    def service(j, s):
        for i in range(per_half):
            for d in range(2):
                r = d * per_half + i
                hop_arrived(j, s, r, d)

                @pl.when(s < n - 1)
                def _():
                    hop(j, s, r, d).start()

    for j in range(kvl):
        for k in range(1, heads):
            for copy in cross_kv(j, k):
                copy.start()
    for j in range(kvl):
        for copy in local_kv(j):
            copy.start()
    for j in range(kvl):
        for k in range(1, heads):
            cross_q(j, k).start()
    for j in range(kvl):
        local_q(j).start()

    @pl.when(sec == 0)
    def _():
        local_base().start()

    for copy in local_probe():
        copy.start()

    maxima[...] = jnp.full_like(maxima, LOW)
    totals[...] = jnp.zeros_like(totals)
    squares[...] = jnp.zeros_like(squares)
    products[...] = jnp.zeros_like(products)
    accs[n // 2] = jnp.zeros_like(accs[n // 2])

    lower = jnp.int32(0)
    for b in range(n):
        lower = jnp.where(me == b, order_ref[b], lower)
    lower_steps = (lower + 2) // 2
    scale = math.log2(math.e) / math.sqrt(HEAD_DIM)
    pairs = max(1, group // 2)
    lanes = group * span // pairs
    heads_in = lanes // span

    def where_is(c):
        first = jnp.minimum(c, 2 * n - 1 - c)
        b = jnp.int32(0)
        for i in range(n):
            b = jnp.where(order_ref[i] == first, i, b)
        return b, jnp.where(c < n, 0, 1)

    def turn(j):
        for half in range(2):
            for g in range(group):
                at = slice(g * HEAD_DIM, (g + 1) * HEAD_DIM)
                turned[half, :, g * span : (g + 1) * span] = qbufs[j][half, :, at].T

    def chunk(j, t):
        in_lower = t < lower_steps
        half = jnp.where(in_lower, 0, 1)
        own = jnp.where(in_lower, lower, 2 * n - 1 - lower)
        key = jnp.where(in_lower, t, t - lower_steps)
        fresh = jnp.logical_or(t == 0, t == lower_steps)
        b0, h0 = where_is(2 * key)
        b1, h1 = where_is(2 * key + 1)
        kv0 = kvbufs[j][b0, h0]
        kv1 = kvbufs[j][b1, h1]
        keys = jnp.concatenate([kv0[:, :HEAD_DIM], kv1[:, :HEAD_DIM]], axis=0)
        values = jnp.concatenate([kv0[:, HEAD_DIM:], kv1[:, HEAD_DIM:]], axis=0).T
        limit = (own - 2 * key) * span
        ahead = lax.broadcasted_iota(jnp.int32, (2 * span, span), 0) - lax.broadcasted_iota(
            jnp.int32, (2 * span, span), 1
        )
        seen = jnp.concatenate([ahead <= limit] * heads_in, axis=1)
        before = jnp.where(t == 0, n // 2, jnp.minimum(t - 1, n // 2))
        now = jnp.minimum(t, n // 2)
        old_max = jnp.where(fresh, LOW, maxima[before])
        old_total = totals[before]

        def at(p):
            return slice(p * lanes, (p + 1) * lanes)

        def scores_of(p):
            return jnp.dot(keys, turned[half, :, at(p)], preferred_element_type=jnp.float32)

        def soften(p, scores):
            scores = jnp.where(seen, scores, LOW)
            new_max = jnp.maximum(old_max[:, at(p)], jnp.max(scores, axis=0, keepdims=True))
            weights = jnp.exp2((scores - new_max) * scale)
            fade = jnp.exp2((old_max[:, at(p)] - new_max) * scale)
            total = old_total[:, at(p)] * fade + jnp.sum(weights, axis=0, keepdims=True)
            mixed = jnp.dot(
                values, weights.astype(jnp.bfloat16), preferred_element_type=jnp.float32
            )
            return new_max, total, fade, mixed

        def keep(p, results):
            new_max, total, fade, mixed = results
            accs[now, :, at(p)] = accs[before, :, at(p)] * fade + mixed
            maxima[now, :, at(p)] = new_max
            totals[now, :, at(p)] = total

        coming = scores_of(0)
        held = None
        for p in range(pairs):
            scores = coming
            if p + 1 < pairs:
                coming = scores_of(p + 1)
            results = soften(p, scores)
            if held is not None:
                keep(p - 1, held)
            held = results
        keep(pairs - 1, held)

    def hand(j):
        piece = base.at[:, pl.ds(pl.multiple_of(j * width, width), width)]
        return pltpu.make_async_remote_copy(
            src_ref=out_ref.at[0, :, pl.ds(pl.multiple_of(j * width, width), width)],
            dst_ref=piece,
            send_sem=hand_send.at[j],
            recv_sem=hand_recv.at[j],
            device_id={"section": 1 - sec},
            device_id_type=MESH,
        )

    def finish(j):
        if j == 0:

            @pl.when(sec == 0)
            def _():
                local_base().wait()

            for copy in local_probe():
                copy.wait()

        @pl.when(sec == 1)
        def _():
            hand(j).wait_recv()

        for half in range(2):
            slot = lower_steps - 1 if half == 0 else n // 2
            inverse = 1.0 / totals[slot]
            for g in range(group):
                at = slice(g * span, (g + 1) * span)
                cols = pl.ds(pl.multiple_of(j * width + g * HEAD_DIM, HEAD_DIM), HEAD_DIM)
                r = slice(half * span, (half + 1) * span)
                attended = (accs[slot, :, at] * inverse[:, at]).T
                stream = (base[r, cols].astype(jnp.float32) + attended).astype(jnp.bfloat16)
                out_ref[0, r, cols] = stream
                wide = stream.astype(jnp.float32)
                squares[half] += wide * wide
                products[half] += wide * (gain_ref[:, cols] * weight_ref[:, cols])

        @pl.when(sec == 0)
        def _():
            hand(j).start()

    stagger = max(1, (n - 1) // 3)
    first_hops(0)

    def slot(time, carry):
        for j in range(kvl):
            s = time - j * stagger

            @pl.when(jnp.logical_and(s >= 1, s < n))
            def _():
                service(j, s)

            if j:

                @pl.when(s == 0)
                def _():
                    first_hops(j)

        return carry

    lax.fori_loop(1, n, slot, 0)
    for j in range(kvl):
        queries_here(j)
        turn(j)
        later = kvl - 1 - j
        apart = max(1, steps // max(1, later * stagger))

        def one(t, carry, j=j, later=later, apart=apart):
            chunk(j, t)
            for i in range(later):
                turn_of = (t + 1) // apart - 1

                @pl.when(
                    jnp.logical_and((t + 1) % apart == 0, turn_of % later == i)
                )
                def _():
                    s = n + j * stagger + turn_of // later - (j + 1 + i) * stagger

                    @pl.when(jnp.logical_and(s >= 1, turn_of < later * stagger))
                    def _():
                        service(j + 1 + i, s)

                    if i:

                        @pl.when(jnp.logical_and(s == 0, turn_of < later * stagger))
                        def _():
                            first_hops(j + 1 + i)

            return carry

        lax.fori_loop(0, steps, one, 0)
        for i in range(steps // apart, later * stagger):
            s = n + j * stagger + i // later - (j + 1 + i % later) * stagger
            if s >= 1:
                service(j + 1 + i % later, s)
            elif s == 0:
                first_hops(j + 1 + i % later)
        finish(j)

    def totals_of(ref):
        return [jnp.sum(ref[half].T, axis=0, keepdims=True) for half in range(2)]

    parts[h] = jnp.concatenate(totals_of(squares) + totals_of(products), axis=0)

    def share(k):
        return pltpu.make_async_remote_copy(
            src_ref=parts.at[h],
            dst_ref=parts.at[h],
            send_sem=part_send.at[k],
            recv_sem=part_recv.at[k],
            device_id={"head": (h + k) % heads},
            device_id_type=MESH,
        )

    for k in range(1, heads):
        share(k).start()
    for k in range(1, heads):
        piece = parts.at[(h + heads - k) % heads]
        pltpu.make_async_copy(piece, piece, part_recv.at[k]).wait()
    both = parts[0]
    for k in range(1, heads):
        both = both + parts[k]
    features = heads * kvl * width
    reward = both[2:4] * lax.rsqrt(both[0:2] / features + 1e-05)
    reward_ref[...] = jnp.concatenate([reward[:1], reward[1:]], axis=1)

    for k in range(1, heads):
        share(k).wait_send()
        for j in range(kvl):
            for copy in cross_kv(j, k):
                copy.wait_send()
            cross_q(j, k).wait_send()
    for j in range(kvl):

        def sent(s, carry, j=j):
            for r in range(heads):
                hop(j, s, r, r // per_half).wait_send()
            return carry

        lax.fori_loop(0, n - 1, sent, 0)

    @pl.when(sec == 0)
    def _():
        for j in range(kvl):
            hand(j).wait_send()


def body(queries, key_vectors, value_vectors, residual, pair_order, probe_gain, probe_weight):
    n = lax.axis_size("blk")
    heads = lax.axis_size("head")
    rows, features = queries.shape[1:]
    kvl = key_vectors.shape[2] // HEAD_DIM // heads
    group = features // key_vectors.shape[2]
    span = residual.shape[0] // 2
    width = group * HEAD_DIM
    local = residual.shape[1]
    sizes = (n, heads, kvl, group, span, rows)
    dma = pltpu.SemaphoreType.DMA
    hbm = pl.BlockSpec(memory_space=pltpu.HBM)
    vmem = pl.BlockSpec(memory_space=pltpu.VMEM)
    slots = n // 2 + 1
    stream, reward = pl.pallas_call(
        functools.partial(kernel, sizes),
        out_shape=(
            jax.ShapeDtypeStruct((1, 2 * span, local), jnp.bfloat16),
            jax.ShapeDtypeStruct((1, 2 * span), jnp.float32),
        ),
        in_specs=[pl.BlockSpec(memory_space=pltpu.SMEM)] + [hbm] * 6,
        out_specs=(vmem, vmem),
        scratch_shapes=[
            [pltpu.VMEM((n, 2, span, 2 * HEAD_DIM), jnp.bfloat16)] * kvl,
            [pltpu.VMEM((2, span, width), jnp.bfloat16)] * kvl,
            pltpu.VMEM((2, HEAD_DIM, group * span), jnp.bfloat16),
            pltpu.VMEM((2 * span, local), jnp.bfloat16),
            pltpu.VMEM((1, local), jnp.float32),
            pltpu.VMEM((1, local), jnp.float32),
            pltpu.VMEM((slots, HEAD_DIM, group * span), jnp.float32),
            pltpu.VMEM((slots, 1, group * span), jnp.float32),
            pltpu.VMEM((slots, 1, group * span), jnp.float32),
            pltpu.VMEM((2, span, HEAD_DIM), jnp.float32),
            pltpu.VMEM((2, span, HEAD_DIM), jnp.float32),
            pltpu.VMEM((heads, 4, span), jnp.float32),
            dma((3, kvl)),
            dma((3,)),
            dma((2, kvl, heads)),
            dma((2, kvl, heads)),
            dma((kvl, heads)),
            dma((kvl, heads)),
            dma((kvl, n, heads)),
            dma((kvl, n, heads)),
            dma((kvl,)),
            dma((kvl,)),
            dma((heads,)),
            dma((heads,)),
        ],
        compiler_params=pltpu.CompilerParams(
            collective_id=0, has_side_effects=True, vmem_limit_bytes=58 * 1024 * 1024
        ),
        name="attention",
    )(pair_order, queries[0], key_vectors[0], value_vectors[0], residual, probe_gain, probe_weight)
    return stream, reward


def solution(mesh):
    return jax.shard_map(
        body,
        mesh=mesh,
        in_specs=(
            P("section", ("blk", "head"), None),
            P("section", ("blk", "head"), None),
            P("section", ("blk", "head"), None),
            P("blk", "head"),
            P(),
            P("section", "head"),
            P("section", "head"),
        ),
        out_specs=(P("section", "blk", "head"), P("section", "blk")),
        check_vma=False,
    )
```

```python
import functools
import math

import jax
import jax.numpy as jnp
from jax import lax
from jax.experimental import pallas as pl
from jax.experimental.pallas import tpu as pltpu
from jax.sharding import PartitionSpec as P

HEAD_DIM = 128
LOW = -1e30
ONES = 16
MESH = pl.DeviceIdType.MESH


def kernel(
    sizes,
    order_ref,
    q_ref,
    k_ref,
    v_ref,
    res_ref,
    gain_hbm,
    weight_hbm,
    out_ref,
    reward_ref,
    kvbufs,
    qbufs,
    turned,
    base,
    gain_ref,
    weight_ref,
    accs,
    maxima,
    squares,
    products,
    parts,
    local_sem,
    base_sem,
    xkv_send,
    xkv_recv,
    xq_send,
    xq_recv,
    ring_send,
    ring_recv,
    hand_send,
    hand_recv,
    part_send,
    part_recv,
):
    n, heads, kvl, group, span, rows = sizes
    steps = n + 1
    width = group * HEAD_DIM
    per_half = heads // 2
    sec = lax.axis_index("section")
    me = lax.axis_index("blk")
    h = lax.axis_index("head")

    def index_of(place):
        return jnp.where(2 * place < n, 2 * place, 2 * (n - 1 - place) + 1)

    place = jnp.where(me % 2 == 0, me // 2, n - 1 - me // 2)
    right = index_of((place + 1) % n)
    left = index_of((place + n - 1) % n)

    barrier = pltpu.get_barrier_semaphore()
    for to in (left, right):
        pl.semaphore_signal(barrier, inc=1, device_id={"blk": to}, device_id_type=MESH)
    for k in range(1, heads):
        pl.semaphore_signal(barrier, inc=1, device_id={"head": (h + k) % heads}, device_id_type=MESH)
    pl.semaphore_signal(barrier, inc=1, device_id={"section": 1 - sec}, device_id_type=MESH)
    pl.semaphore_wait(barrier, heads + 2)

    def rows_of(source):
        return source // per_half, pl.ds(pl.multiple_of((source % per_half) * rows, rows), rows)

    half_own, at_own = rows_of(h)

    def local_kv(j):
        cols = pl.ds(pl.multiple_of((h * kvl + j) * HEAD_DIM, HEAD_DIM), HEAD_DIM)
        return [
            pltpu.make_async_copy(
                ref.at[:, cols],
                kvbufs[j].at[me, half_own, at_own, pl.ds(i * HEAD_DIM, HEAD_DIM)],
                local_sem.at[i, j],
            )
            for i, ref in enumerate((k_ref, v_ref))
        ]

    def local_q(j):
        cols = pl.ds(pl.multiple_of((h * kvl + j) * width, width), width)
        return pltpu.make_async_copy(
            q_ref.at[:, cols], qbufs[j].at[half_own, at_own, :], local_sem.at[2, j]
        )

    def local_base():
        return pltpu.make_async_copy(res_ref, base, base_sem.at[0])

    def local_probe():
        return [
            pltpu.make_async_copy(gain_hbm, gain_ref, base_sem.at[1]),
            pltpu.make_async_copy(weight_hbm, weight_ref, base_sem.at[2]),
        ]

    def cross_kv(j, k):
        to = (h + k) % heads
        cols = pl.ds(pl.multiple_of((to * kvl + j) * HEAD_DIM, HEAD_DIM), HEAD_DIM)
        return [
            pltpu.make_async_remote_copy(
                src_ref=ref.at[:, cols],
                dst_ref=kvbufs[j].at[me, half_own, at_own, pl.ds(i * HEAD_DIM, HEAD_DIM)],
                send_sem=xkv_send.at[i, j, k],
                recv_sem=xkv_recv.at[i, j, k],
                device_id={"head": to},
                device_id_type=MESH,
            )
            for i, ref in enumerate((k_ref, v_ref))
        ]

    def cross_kv_arrived(j, k):
        half, at = rows_of((h + heads - k) % heads)
        for i in range(2):
            piece = kvbufs[j].at[me, half, at, pl.ds(i * HEAD_DIM, HEAD_DIM)]
            pltpu.make_async_copy(piece, piece, xkv_recv.at[i, j, k]).wait()

    def cross_q(j, k):
        to = (h + k) % heads
        cols = pl.ds(pl.multiple_of((to * kvl + j) * width, width), width)
        return pltpu.make_async_remote_copy(
            src_ref=q_ref.at[:, cols],
            dst_ref=qbufs[j].at[half_own, at_own, :],
            send_sem=xq_send.at[j, k],
            recv_sem=xq_recv.at[j, k],
            device_id={"head": to},
            device_id_type=MESH,
        )

    def queries_here(j):
        local_q(j).wait()
        for k in range(1, heads):
            half, at = rows_of((h + heads - k) % heads)
            piece = qbufs[j].at[half, at, :]
            pltpu.make_async_copy(piece, piece, xq_recv.at[j, k]).wait()

    def piece_of(j, s, r, d):
        away = (place + n - s) % n if d == 0 else (place + s) % n
        half, at = rows_of(r)
        return kvbufs[j].at[index_of(away), half, at, :]

    def hop(j, s, r, d):
        piece = piece_of(j, s, r, d)
        return pltpu.make_async_remote_copy(
            src_ref=piece,
            dst_ref=piece,
            send_sem=ring_send.at[j, s, r],
            recv_sem=ring_recv.at[j, s, r],
            device_id={"blk": right if d == 0 else left},
            device_id_type=MESH,
        )

    def hop_arrived(j, s, r, d):
        piece = piece_of(j, s, r, d)
        pltpu.make_async_copy(piece, piece, ring_recv.at[j, s - 1, r]).wait()

    def first_hop(j, r):
        @pl.when(r < per_half)
        def _():
            hop(j, 0, r, 0).start()

        @pl.when(r >= per_half)
        def _():
            hop(j, 0, r, 1).start()

    def first_hops(j):
        for copy in local_kv(j):
            copy.wait()
        first_hop(j, h)
        for k in range(1, heads):
            cross_kv_arrived(j, k)
            first_hop(j, (h + heads - k) % heads)

    def service(j, s):
        for i in range(per_half):
            for d in range(2):
                r = d * per_half + i
                hop_arrived(j, s, r, d)

                @pl.when(s < n - 1)
                def _():
                    hop(j, s, r, d).start()

    for j in range(kvl):
        for k in range(1, heads):
            for copy in cross_kv(j, k):
                copy.start()
    for j in range(kvl):
        for copy in local_kv(j):
            copy.start()
    for j in range(kvl):
        for k in range(1, heads):
            cross_q(j, k).start()
    for j in range(kvl):
        local_q(j).start()

    @pl.when(sec == 0)
    def _():
        local_base().start()

    for copy in local_probe():
        copy.start()

    maxima[...] = jnp.full_like(maxima, LOW)
    squares[...] = jnp.zeros_like(squares)
    products[...] = jnp.zeros_like(products)
    accs[n // 2] = jnp.zeros_like(accs[n // 2])
    ones = jnp.ones((ONES, 2 * span), jnp.bfloat16)

    lower = jnp.int32(0)
    for b in range(n):
        lower = jnp.where(me == b, order_ref[b], lower)
    upper_steps = steps - (lower + 2) // 2
    scale = math.log2(math.e) / math.sqrt(HEAD_DIM)
    pairs = max(1, group // 2)
    lanes = group * span // pairs
    heads_in = lanes // span

    def where_is(c):
        first = jnp.minimum(c, 2 * n - 1 - c)
        b = jnp.int32(0)
        for i in range(n):
            b = jnp.where(order_ref[i] == first, i, b)
        return b, jnp.where(c < n, 0, 1)

    def turn(j):
        for half in range(2):
            for g in range(group):
                at = slice(g * HEAD_DIM, (g + 1) * HEAD_DIM)
                turned[half, :, g * span : (g + 1) * span] = qbufs[j][half, :, at].T

    def slot_of(t):
        return jnp.maximum(t - n // 2, 0)

    def chunk(j, t, masked):
        in_upper = t < upper_steps
        half = jnp.where(in_upper, 1, 0)
        own = jnp.where(in_upper, 2 * n - 1 - lower, lower)
        key = jnp.where(in_upper, upper_steps - 1 - t, t - upper_steps)
        fresh = jnp.logical_or(t == 0, t == upper_steps)
        b0, h0 = where_is(2 * key)
        b1, h1 = where_is(2 * key + 1)
        kv0 = kvbufs[j][b0, h0]
        kv1 = kvbufs[j][b1, h1]
        keys = jnp.concatenate([kv0[:, :HEAD_DIM], kv1[:, :HEAD_DIM]], axis=0)
        values = jnp.concatenate([kv0[:, HEAD_DIM:], kv1[:, HEAD_DIM:]], axis=0).T
        values = jnp.concatenate([values, ones], axis=0)
        if masked:
            limit = (own - 2 * key) * span
            ahead = lax.broadcasted_iota(jnp.int32, (2 * span, span), 0) - lax.broadcasted_iota(
                jnp.int32, (2 * span, span), 1
            )
            seen = jnp.concatenate([ahead <= limit] * heads_in, axis=1)
        before = jnp.where(t == 0, n // 2, slot_of(t - 1))
        now = slot_of(t)
        old_max = jnp.where(fresh, LOW, maxima[before])

        def at(p):
            return slice(p * lanes, (p + 1) * lanes)

        def scores_of(p):
            return jnp.dot(keys, turned[half, :, at(p)], preferred_element_type=jnp.float32)

        def soften(p, scores):
            if masked:
                scores = jnp.where(seen, scores, LOW)
            new_max = jnp.maximum(old_max[:, at(p)], jnp.max(scores, axis=0, keepdims=True))
            weights = jnp.exp2(((scores - new_max) * scale).astype(jnp.bfloat16))
            fade = jnp.exp2((old_max[:, at(p)] - new_max) * scale)
            return new_max, fade, jnp.dot(values, weights, preferred_element_type=jnp.float32)

        def keep(p, results):
            new_max, fade, mixed = results
            accs[now, :, at(p)] = accs[before, :, at(p)] * fade + mixed
            maxima[now, :, at(p)] = new_max

        coming = scores_of(0)
        held = None
        for p in range(pairs):
            scores = coming
            if p + 1 < pairs:
                coming = scores_of(p + 1)
            results = soften(p, scores)
            if held is not None:
                keep(p - 1, held)
            held = results
        keep(pairs - 1, held)

    def hand(j):
        piece = base.at[:, pl.ds(pl.multiple_of(j * width, width), width)]
        return pltpu.make_async_remote_copy(
            src_ref=out_ref.at[0, :, pl.ds(pl.multiple_of(j * width, width), width)],
            dst_ref=piece,
            send_sem=hand_send.at[j],
            recv_sem=hand_recv.at[j],
            device_id={"section": 1 - sec},
            device_id_type=MESH,
        )

    def finish(j):
        if j == 0:

            @pl.when(sec == 0)
            def _():
                local_base().wait()

            for copy in local_probe():
                copy.wait()

        @pl.when(sec == 1)
        def _():
            hand(j).wait_recv()

        for half in range(2):
            slot = n // 2 if half == 0 else slot_of(upper_steps - 1)
            inverse = 1.0 / accs[slot, HEAD_DIM : HEAD_DIM + 1, :]
            for g in range(group):
                at = slice(g * span, (g + 1) * span)
                cols = pl.ds(pl.multiple_of(j * width + g * HEAD_DIM, HEAD_DIM), HEAD_DIM)
                r = slice(half * span, (half + 1) * span)
                attended = (accs[slot, :HEAD_DIM, at] * inverse[:, at]).T
                stream = (base[r, cols].astype(jnp.float32) + attended).astype(jnp.bfloat16)
                out_ref[0, r, cols] = stream
                wide = stream.astype(jnp.float32)
                squares[half] += wide * wide
                products[half] += wide * (gain_ref[:, cols] * weight_ref[:, cols])

        @pl.when(sec == 0)
        def _():
            hand(j).start()

    stagger = max(1, (n - 1) // 3)
    first_hops(0)

    def slot(time, carry):
        for j in range(kvl):
            s = time - j * stagger

            @pl.when(jnp.logical_and(s >= 1, s < n))
            def _():
                service(j, s)

            if j:

                @pl.when(s == 0)
                def _():
                    first_hops(j)

        return carry

    lax.fori_loop(1, n, slot, 0)
    for j in range(kvl):
        queries_here(j)
        turn(j)
        later = kvl - 1 - j
        apart = max(1, steps // max(1, later * stagger))

        def one(t, carry, j=j, later=later, apart=apart):
            edge = jnp.logical_or(t == 0, t == steps - 1)

            @pl.when(edge)
            def _():
                chunk(j, t, True)

            @pl.when(jnp.logical_not(edge))
            def _():
                chunk(j, t, False)

            for i in range(later):
                turn_of = (t + 1) // apart - 1

                @pl.when(
                    jnp.logical_and((t + 1) % apart == 0, turn_of % later == i)
                )
                def _():
                    s = n + j * stagger + turn_of // later - (j + 1 + i) * stagger

                    @pl.when(jnp.logical_and(s >= 1, turn_of < later * stagger))
                    def _():
                        service(j + 1 + i, s)

                    if i:

                        @pl.when(jnp.logical_and(s == 0, turn_of < later * stagger))
                        def _():
                            first_hops(j + 1 + i)

            return carry

        lax.fori_loop(0, steps, one, 0)
        for i in range(steps // apart, later * stagger):
            s = n + j * stagger + i // later - (j + 1 + i % later) * stagger
            if s >= 1:
                service(j + 1 + i % later, s)
            elif s == 0:
                first_hops(j + 1 + i % later)
        finish(j)

    def totals_of(ref):
        return [jnp.sum(ref[half].T, axis=0, keepdims=True) for half in range(2)]

    parts[h] = jnp.concatenate(totals_of(squares) + totals_of(products), axis=0)

    def share(k):
        return pltpu.make_async_remote_copy(
            src_ref=parts.at[h],
            dst_ref=parts.at[h],
            send_sem=part_send.at[k],
            recv_sem=part_recv.at[k],
            device_id={"head": (h + k) % heads},
            device_id_type=MESH,
        )

    for k in range(1, heads):
        share(k).start()
    for k in range(1, heads):
        piece = parts.at[(h + heads - k) % heads]
        pltpu.make_async_copy(piece, piece, part_recv.at[k]).wait()
    both = parts[0]
    for k in range(1, heads):
        both = both + parts[k]
    features = heads * kvl * width
    reward = both[2:4] * lax.rsqrt(both[0:2] / features + 1e-05)
    reward_ref[...] = jnp.concatenate([reward[:1], reward[1:]], axis=1)

    for k in range(1, heads):
        share(k).wait_send()
        for j in range(kvl):
            for copy in cross_kv(j, k):
                copy.wait_send()
            cross_q(j, k).wait_send()
    for j in range(kvl):

        def sent(s, carry, j=j):
            for r in range(heads):
                hop(j, s, r, r // per_half).wait_send()
            return carry

        lax.fori_loop(0, n - 1, sent, 0)

    @pl.when(sec == 0)
    def _():
        for j in range(kvl):
            hand(j).wait_send()


def body(queries, key_vectors, value_vectors, residual, pair_order, probe_gain, probe_weight):
    n = lax.axis_size("blk")
    heads = lax.axis_size("head")
    rows, features = queries.shape[1:]
    kvl = key_vectors.shape[2] // HEAD_DIM // heads
    group = features // key_vectors.shape[2]
    span = residual.shape[0] // 2
    width = group * HEAD_DIM
    local = residual.shape[1]
    sizes = (n, heads, kvl, group, span, rows)
    dma = pltpu.SemaphoreType.DMA
    hbm = pl.BlockSpec(memory_space=pltpu.HBM)
    vmem = pl.BlockSpec(memory_space=pltpu.VMEM)
    slots = n // 2 + 1
    stream, reward = pl.pallas_call(
        functools.partial(kernel, sizes),
        out_shape=(
            jax.ShapeDtypeStruct((1, 2 * span, local), jnp.bfloat16),
            jax.ShapeDtypeStruct((1, 2 * span), jnp.float32),
        ),
        in_specs=[pl.BlockSpec(memory_space=pltpu.SMEM)] + [hbm] * 6,
        out_specs=(vmem, vmem),
        scratch_shapes=[
            [pltpu.VMEM((n, 2, span, 2 * HEAD_DIM), jnp.bfloat16)] * kvl,
            [pltpu.VMEM((2, span, width), jnp.bfloat16)] * kvl,
            pltpu.VMEM((2, HEAD_DIM, group * span), jnp.bfloat16),
            pltpu.VMEM((2 * span, local), jnp.bfloat16),
            pltpu.VMEM((1, local), jnp.float32),
            pltpu.VMEM((1, local), jnp.float32),
            pltpu.VMEM((slots, HEAD_DIM + ONES, group * span), jnp.float32),
            pltpu.VMEM((slots, 1, group * span), jnp.float32),
            pltpu.VMEM((2, span, HEAD_DIM), jnp.float32),
            pltpu.VMEM((2, span, HEAD_DIM), jnp.float32),
            pltpu.VMEM((heads, 4, span), jnp.float32),
            dma((3, kvl)),
            dma((3,)),
            dma((2, kvl, heads)),
            dma((2, kvl, heads)),
            dma((kvl, heads)),
            dma((kvl, heads)),
            dma((kvl, n, heads)),
            dma((kvl, n, heads)),
            dma((kvl,)),
            dma((kvl,)),
            dma((heads,)),
            dma((heads,)),
        ],
        compiler_params=pltpu.CompilerParams(
            collective_id=0, has_side_effects=True, vmem_limit_bytes=58 * 1024 * 1024
        ),
        name="attention",
    )(pair_order, queries[0], key_vectors[0], value_vectors[0], residual, probe_gain, probe_weight)
    return stream, reward


def solution(mesh):
    return jax.shard_map(
        body,
        mesh=mesh,
        in_specs=(
            P("section", ("blk", "head"), None),
            P("section", ("blk", "head"), None),
            P("section", ("blk", "head"), None),
            P("blk", "head"),
            P(),
            P("section", "head"),
            P("section", "head"),
        ),
        out_specs=(P("section", "blk", "head"), P("section", "blk")),
        check_vma=False,
    )
```

```python
import functools
import math

import jax
import jax.numpy as jnp
from jax import lax
from jax.experimental import pallas as pl
from jax.experimental.pallas import tpu as pltpu
from jax.sharding import PartitionSpec as P

HEAD_DIM = 128
LOW = -1e30
ONES = 16
MESH = pl.DeviceIdType.MESH


def kernel(
    sizes,
    order_ref,
    q_ref,
    k_ref,
    v_ref,
    res_ref,
    gain_hbm,
    weight_hbm,
    out_ref,
    reward_ref,
    kvbufs,
    qbufs,
    turned,
    base,
    gain_ref,
    weight_ref,
    accs,
    maxima,
    squares,
    products,
    parts,
    local_sem,
    base_sem,
    xkv_send,
    xkv_recv,
    xq_send,
    xq_recv,
    ring_send,
    ring_recv,
    hand_send,
    hand_recv,
    part_send,
    part_recv,
):
    n, heads, kvl, group, span, rows = sizes
    steps = n + 1
    width = group * HEAD_DIM
    per_half = heads // 2
    sec = lax.axis_index("section")
    me = lax.axis_index("blk")
    h = lax.axis_index("head")

    def index_of(place):
        return jnp.where(2 * place < n, 2 * place, 2 * (n - 1 - place) + 1)

    place = jnp.where(me % 2 == 0, me // 2, n - 1 - me // 2)
    right = index_of((place + 1) % n)
    left = index_of((place + n - 1) % n)

    barrier = pltpu.get_barrier_semaphore()
    for to in (left, right):
        pl.semaphore_signal(barrier, inc=1, device_id={"blk": to}, device_id_type=MESH)
    for k in range(1, heads):
        pl.semaphore_signal(barrier, inc=1, device_id={"head": (h + k) % heads}, device_id_type=MESH)
    pl.semaphore_signal(barrier, inc=1, device_id={"section": 1 - sec}, device_id_type=MESH)
    pl.semaphore_wait(barrier, heads + 2)

    def rows_of(source):
        return source // per_half, pl.ds(pl.multiple_of((source % per_half) * rows, rows), rows)

    half_own, at_own = rows_of(h)

    def local_kv(j):
        cols = pl.ds(pl.multiple_of((h * kvl + j) * HEAD_DIM, HEAD_DIM), HEAD_DIM)
        return [
            pltpu.make_async_copy(
                ref.at[:, cols],
                kvbufs[j].at[me, half_own, at_own, pl.ds(i * HEAD_DIM, HEAD_DIM)],
                local_sem.at[i, j],
            )
            for i, ref in enumerate((k_ref, v_ref))
        ]

    def local_q(j):
        cols = pl.ds(pl.multiple_of((h * kvl + j) * width, width), width)
        return pltpu.make_async_copy(
            q_ref.at[:, cols], qbufs[j].at[half_own, at_own, :], local_sem.at[2, j]
        )

    def local_base():
        return pltpu.make_async_copy(res_ref, base, base_sem.at[0])

    def local_probe():
        return [
            pltpu.make_async_copy(gain_hbm, gain_ref, base_sem.at[1]),
            pltpu.make_async_copy(weight_hbm, weight_ref, base_sem.at[2]),
        ]

    def cross_kv(j, k):
        to = (h + k) % heads
        cols = pl.ds(pl.multiple_of((to * kvl + j) * HEAD_DIM, HEAD_DIM), HEAD_DIM)
        return [
            pltpu.make_async_remote_copy(
                src_ref=ref.at[:, cols],
                dst_ref=kvbufs[j].at[me, half_own, at_own, pl.ds(i * HEAD_DIM, HEAD_DIM)],
                send_sem=xkv_send.at[i, j, k],
                recv_sem=xkv_recv.at[i, j, k],
                device_id={"head": to},
                device_id_type=MESH,
            )
            for i, ref in enumerate((k_ref, v_ref))
        ]

    def cross_kv_arrived(j, k):
        half, at = rows_of((h + heads - k) % heads)
        for i in range(2):
            piece = kvbufs[j].at[me, half, at, pl.ds(i * HEAD_DIM, HEAD_DIM)]
            pltpu.make_async_copy(piece, piece, xkv_recv.at[i, j, k]).wait()

    def cross_q(j, k):
        to = (h + k) % heads
        cols = pl.ds(pl.multiple_of((to * kvl + j) * width, width), width)
        return pltpu.make_async_remote_copy(
            src_ref=q_ref.at[:, cols],
            dst_ref=qbufs[j].at[half_own, at_own, :],
            send_sem=xq_send.at[j, k],
            recv_sem=xq_recv.at[j, k],
            device_id={"head": to},
            device_id_type=MESH,
        )

    def queries_here(j):
        local_q(j).wait()
        for k in range(1, heads):
            half, at = rows_of((h + heads - k) % heads)
            piece = qbufs[j].at[half, at, :]
            pltpu.make_async_copy(piece, piece, xq_recv.at[j, k]).wait()

    def reach(j, d):
        return n // 2 if j % 2 == d else (n - 1) // 2

    def piece_of(j, s, r, d):
        away = (place + n - s) % n if d == 0 else (place + s) % n
        half, at = rows_of(r)
        return kvbufs[j].at[index_of(away), half, at, :]

    def hop(j, s, r, d):
        piece = piece_of(j, s, r, d)
        return pltpu.make_async_remote_copy(
            src_ref=piece,
            dst_ref=piece,
            send_sem=ring_send.at[j, d, s, r],
            recv_sem=ring_recv.at[j, d, s, r],
            device_id={"blk": right if d == 0 else left},
            device_id_type=MESH,
        )

    def first_hop(j, r):
        for d in range(2):
            if reach(j, d) > 0:
                hop(j, 0, r, d).start()

    def first_hops(j):
        for copy in local_kv(j):
            copy.wait()
        first_hop(j, h)
        for k in range(1, heads):
            cross_kv_arrived(j, k)
            first_hop(j, (h + heads - k) % heads)

    def service(j, s):
        for k in range(heads):
            r = (h + heads - k) % heads
            for d in range(2):

                @pl.when(s <= reach(j, d))
                def _():
                    piece = piece_of(j, s, r, d)
                    pltpu.make_async_copy(piece, piece, ring_recv.at[j, d, s - 1, r]).wait()

                @pl.when(s < reach(j, d))
                def _():
                    hop(j, s, r, d).start()

    for j in range(kvl):
        for k in range(1, heads):
            for copy in cross_kv(j, k):
                copy.start()
    for j in range(kvl):
        for copy in local_kv(j):
            copy.start()
    early = max(1, kvl // 2)
    for j in range(early):
        for k in range(1, heads):
            cross_q(j, k).start()
    for j in range(kvl):
        local_q(j).start()

    @pl.when(sec == 0)
    def _():
        local_base().start()

    for copy in local_probe():
        copy.start()

    maxima[...] = jnp.full_like(maxima, LOW)
    squares[...] = jnp.zeros_like(squares)
    products[...] = jnp.zeros_like(products)
    accs[n // 2] = jnp.zeros_like(accs[n // 2])
    ones = jnp.ones((ONES, 2 * span), jnp.bfloat16)

    lower = jnp.int32(0)
    for b in range(n):
        lower = jnp.where(me == b, order_ref[b], lower)
    upper_steps = steps - (lower + 2) // 2
    scale = math.log2(math.e) / math.sqrt(HEAD_DIM)
    pairs = max(1, group // 2)
    lanes = group * span // pairs
    heads_in = lanes // span

    def where_is(c):
        first = jnp.minimum(c, 2 * n - 1 - c)
        b = jnp.int32(0)
        for i in range(n):
            b = jnp.where(order_ref[i] == first, i, b)
        return b, jnp.where(c < n, 0, 1)

    def turn(j):
        for half in range(2):
            for g in range(group):
                at = slice(g * HEAD_DIM, (g + 1) * HEAD_DIM)
                turned[half, :, g * span : (g + 1) * span] = qbufs[j][half, :, at].T

    def slot_of(t):
        return jnp.maximum(t - n // 2, 0)

    def chunk(j, t, masked):
        in_upper = t < upper_steps
        half = jnp.where(in_upper, 1, 0)
        own = jnp.where(in_upper, 2 * n - 1 - lower, lower)
        key = jnp.where(in_upper, upper_steps - 1 - t, t - upper_steps)
        fresh = jnp.logical_or(t == 0, t == upper_steps)
        b0, h0 = where_is(2 * key)
        b1, h1 = where_is(2 * key + 1)
        kv0 = kvbufs[j][b0, h0]
        kv1 = kvbufs[j][b1, h1]
        keys = jnp.concatenate([kv0[:, :HEAD_DIM], kv1[:, :HEAD_DIM]], axis=0)
        values = jnp.concatenate([kv0[:, HEAD_DIM:], kv1[:, HEAD_DIM:]], axis=0).T
        values = jnp.concatenate([values, ones], axis=0)
        if masked:
            limit = (own - 2 * key) * span
            ahead = lax.broadcasted_iota(jnp.int32, (2 * span, span), 0) - lax.broadcasted_iota(
                jnp.int32, (2 * span, span), 1
            )
            seen = jnp.concatenate([ahead <= limit] * heads_in, axis=1)
        before = jnp.where(t == 0, n // 2, slot_of(t - 1))
        now = slot_of(t)
        old_max = jnp.where(fresh, LOW, maxima[before])

        def at(p):
            return slice(p * lanes, (p + 1) * lanes)

        def scores_of(p):
            return jnp.dot(keys, turned[half, :, at(p)], preferred_element_type=jnp.float32)

        def soften(p, scores):
            if masked:
                scores = jnp.where(seen, scores, LOW)
            new_max = jnp.maximum(old_max[:, at(p)], jnp.max(scores, axis=0, keepdims=True))
            weights = jnp.exp2(((scores - new_max) * scale).astype(jnp.bfloat16))
            fade = jnp.exp2((old_max[:, at(p)] - new_max) * scale)
            return new_max, fade, jnp.dot(values, weights, preferred_element_type=jnp.float32)

        def keep(p, results):
            new_max, fade, mixed = results
            accs[now, :, at(p)] = accs[before, :, at(p)] * fade + mixed
            maxima[now, :, at(p)] = new_max

        coming = scores_of(0)
        held = None
        for p in range(pairs):
            scores = coming
            if p + 1 < pairs:
                coming = scores_of(p + 1)
            results = soften(p, scores)
            if held is not None:
                keep(p - 1, held)
            held = results
        keep(pairs - 1, held)

    def hand(j):
        piece = base.at[:, pl.ds(pl.multiple_of(j * width, width), width)]
        return pltpu.make_async_remote_copy(
            src_ref=out_ref.at[0, :, pl.ds(pl.multiple_of(j * width, width), width)],
            dst_ref=piece,
            send_sem=hand_send.at[j],
            recv_sem=hand_recv.at[j],
            device_id={"section": 1 - sec},
            device_id_type=MESH,
        )

    def finish(j):
        if j == 0:

            @pl.when(sec == 0)
            def _():
                local_base().wait()

            for copy in local_probe():
                copy.wait()

        @pl.when(sec == 1)
        def _():
            hand(j).wait_recv()

        for half in range(2):
            slot = n // 2 if half == 0 else slot_of(upper_steps - 1)
            inverse = 1.0 / accs[slot, HEAD_DIM : HEAD_DIM + 1, :]
            for g in range(group):
                at = slice(g * span, (g + 1) * span)
                cols = pl.ds(pl.multiple_of(j * width + g * HEAD_DIM, HEAD_DIM), HEAD_DIM)
                r = slice(half * span, (half + 1) * span)
                attended = (accs[slot, :HEAD_DIM, at] * inverse[:, at]).T
                stream = (base[r, cols].astype(jnp.float32) + attended).astype(jnp.bfloat16)
                out_ref[0, r, cols] = stream
                wide = stream.astype(jnp.float32)
                squares[half] += wide * wide
                products[half] += wide * (gain_ref[:, cols] * weight_ref[:, cols])

        @pl.when(sec == 0)
        def _():
            hand(j).start()

    longest = n // 2
    stagger = max(1, longest - 1)
    first_hops(0)

    def slot(time, carry):
        for j in range(kvl):
            s = time - j * stagger

            @pl.when(jnp.logical_and(s >= 1, s <= longest))
            def _():
                service(j, s)

            if j:

                @pl.when(s == 0)
                def _():
                    first_hops(j)

        return carry

    lax.fori_loop(1, longest + 1, slot, 0)
    for j in range(kvl):
        queries_here(j)
        if j == 0:
            for i in range(early, kvl):
                for k in range(1, heads):
                    cross_q(i, k).start()
        turn(j)
        later = kvl - 1 - j
        apart = max(1, steps // max(1, later * stagger))

        def one(t, carry, j=j, later=later, apart=apart):
            edge = jnp.logical_or(t == 0, t == steps - 1)

            @pl.when(edge)
            def _():
                chunk(j, t, True)

            @pl.when(jnp.logical_not(edge))
            def _():
                chunk(j, t, False)

            for i in range(later):
                turn_of = (t + 1) // apart - 1

                @pl.when(
                    jnp.logical_and((t + 1) % apart == 0, turn_of % later == i)
                )
                def _():
                    s = longest + 1 + j * stagger + turn_of // later - (j + 1 + i) * stagger

                    @pl.when(jnp.logical_and(s >= 1, turn_of < later * stagger))
                    def _():
                        service(j + 1 + i, s)

                    if i:

                        @pl.when(jnp.logical_and(s == 0, turn_of < later * stagger))
                        def _():
                            first_hops(j + 1 + i)

            return carry

        lax.fori_loop(0, steps, one, 0)
        for i in range(steps // apart, later * stagger):
            s = longest + 1 + j * stagger + i // later - (j + 1 + i % later) * stagger
            if s >= 1:
                service(j + 1 + i % later, s)
            elif s == 0:
                first_hops(j + 1 + i % later)
        finish(j)

    def totals_of(ref):
        return [jnp.sum(ref[half].T, axis=0, keepdims=True) for half in range(2)]

    parts[h] = jnp.concatenate(totals_of(squares) + totals_of(products), axis=0)

    def share(k):
        return pltpu.make_async_remote_copy(
            src_ref=parts.at[h],
            dst_ref=parts.at[h],
            send_sem=part_send.at[k],
            recv_sem=part_recv.at[k],
            device_id={"head": (h + k) % heads},
            device_id_type=MESH,
        )

    for k in range(1, heads):
        share(k).start()
    for k in range(1, heads):
        piece = parts.at[(h + heads - k) % heads]
        pltpu.make_async_copy(piece, piece, part_recv.at[k]).wait()
    both = parts[0]
    for k in range(1, heads):
        both = both + parts[k]
    features = heads * kvl * width
    reward = both[2:4] * lax.rsqrt(both[0:2] / features + 1e-05)
    reward_ref[...] = jnp.concatenate([reward[:1], reward[1:]], axis=1)

    for k in range(1, heads):
        share(k).wait_send()
        for j in range(kvl):
            for copy in cross_kv(j, k):
                copy.wait_send()
            cross_q(j, k).wait_send()
    for j in range(kvl):

        def sent(s, carry, j=j):
            for r in range(heads):
                for d in range(2):

                    @pl.when(s < reach(j, d))
                    def _():
                        hop(j, s, r, d).wait_send()

            return carry

        lax.fori_loop(0, longest, sent, 0)

    @pl.when(sec == 0)
    def _():
        for j in range(kvl):
            hand(j).wait_send()


def body(queries, key_vectors, value_vectors, residual, pair_order, probe_gain, probe_weight):
    n = lax.axis_size("blk")
    heads = lax.axis_size("head")
    rows, features = queries.shape[1:]
    kvl = key_vectors.shape[2] // HEAD_DIM // heads
    group = features // key_vectors.shape[2]
    span = residual.shape[0] // 2
    width = group * HEAD_DIM
    local = residual.shape[1]
    sizes = (n, heads, kvl, group, span, rows)
    dma = pltpu.SemaphoreType.DMA
    hbm = pl.BlockSpec(memory_space=pltpu.HBM)
    vmem = pl.BlockSpec(memory_space=pltpu.VMEM)
    slots = n // 2 + 1
    stream, reward = pl.pallas_call(
        functools.partial(kernel, sizes),
        out_shape=(
            jax.ShapeDtypeStruct((1, 2 * span, local), jnp.bfloat16),
            jax.ShapeDtypeStruct((1, 2 * span), jnp.float32),
        ),
        in_specs=[pl.BlockSpec(memory_space=pltpu.SMEM)] + [hbm] * 6,
        out_specs=(vmem, vmem),
        scratch_shapes=[
            [pltpu.VMEM((n, 2, span, 2 * HEAD_DIM), jnp.bfloat16)] * kvl,
            [pltpu.VMEM((2, span, width), jnp.bfloat16)] * kvl,
            pltpu.VMEM((2, HEAD_DIM, group * span), jnp.bfloat16),
            pltpu.VMEM((2 * span, local), jnp.bfloat16),
            pltpu.VMEM((1, local), jnp.float32),
            pltpu.VMEM((1, local), jnp.float32),
            pltpu.VMEM((slots, HEAD_DIM + ONES, group * span), jnp.float32),
            pltpu.VMEM((slots, 1, group * span), jnp.float32),
            pltpu.VMEM((2, span, HEAD_DIM), jnp.float32),
            pltpu.VMEM((2, span, HEAD_DIM), jnp.float32),
            pltpu.VMEM((heads, 4, span), jnp.float32),
            dma((3, kvl)),
            dma((3,)),
            dma((2, kvl, heads)),
            dma((2, kvl, heads)),
            dma((kvl, heads)),
            dma((kvl, heads)),
            dma((kvl, 2, n // 2, heads)),
            dma((kvl, 2, n // 2, heads)),
            dma((kvl,)),
            dma((kvl,)),
            dma((heads,)),
            dma((heads,)),
        ],
        compiler_params=pltpu.CompilerParams(
            collective_id=0, has_side_effects=True, vmem_limit_bytes=58 * 1024 * 1024
        ),
        name="attention",
    )(pair_order, queries[0], key_vectors[0], value_vectors[0], residual, probe_gain, probe_weight)
    return stream, reward


def solution(mesh):
    return jax.shard_map(
        body,
        mesh=mesh,
        in_specs=(
            P("section", ("blk", "head"), None),
            P("section", ("blk", "head"), None),
            P("section", ("blk", "head"), None),
            P("blk", "head"),
            P(),
            P("section", "head"),
            P("section", "head"),
        ),
        out_specs=(P("section", "blk", "head"), P("section", "blk")),
        check_vma=False,
    )
```

```python
import functools
import math

import jax
import jax.numpy as jnp
from jax import lax
from jax.experimental import pallas as pl
from jax.experimental.pallas import tpu as pltpu
from jax.sharding import PartitionSpec as P

HEAD_DIM = 128
LOW = -1e30
ONES = 16
MESH = pl.DeviceIdType.MESH


def kernel(
    sizes,
    order_ref,
    q_ref,
    k_ref,
    v_ref,
    res_ref,
    gain_hbm,
    weight_hbm,
    out_ref,
    reward_ref,
    kvbufs,
    qbufs,
    turned,
    base,
    gain_ref,
    weight_ref,
    accs,
    maxima,
    squares,
    products,
    parts,
    local_sem,
    base_sem,
    xkv_send,
    xkv_recv,
    xq_send,
    xq_recv,
    ring_send,
    ring_recv,
    hand_send,
    hand_recv,
    part_send,
    part_recv,
):
    n, heads, kvl, group, span, rows = sizes
    wide = 4 if n % 2 == 0 else 2
    steps = 2 * n // wide + 1
    most_lower = -(-n // wide)
    calm = steps - 1 - most_lower
    width = group * HEAD_DIM
    per_half = heads // 2
    sec = lax.axis_index("section")
    me = lax.axis_index("blk")
    h = lax.axis_index("head")

    def index_of(place):
        return jnp.where(2 * place < n, 2 * place, 2 * (n - 1 - place) + 1)

    place = jnp.where(me % 2 == 0, me // 2, n - 1 - me // 2)
    right = index_of((place + 1) % n)
    left = index_of((place + n - 1) % n)

    barrier = pltpu.get_barrier_semaphore()
    for to in (left, right):
        pl.semaphore_signal(barrier, inc=1, device_id={"blk": to}, device_id_type=MESH)
    for k in range(1, heads):
        pl.semaphore_signal(barrier, inc=1, device_id={"head": (h + k) % heads}, device_id_type=MESH)
    pl.semaphore_signal(barrier, inc=1, device_id={"section": 1 - sec}, device_id_type=MESH)
    pl.semaphore_wait(barrier, heads + 2)

    def rows_of(source):
        return source // per_half, pl.ds(pl.multiple_of((source % per_half) * rows, rows), rows)

    half_own, at_own = rows_of(h)

    def local_kv(j):
        cols = pl.ds(pl.multiple_of((h * kvl + j) * HEAD_DIM, HEAD_DIM), HEAD_DIM)
        return [
            pltpu.make_async_copy(
                ref.at[:, cols],
                kvbufs[j].at[me, half_own, at_own, pl.ds(i * HEAD_DIM, HEAD_DIM)],
                local_sem.at[i, j],
            )
            for i, ref in enumerate((k_ref, v_ref))
        ]

    def local_q(j):
        cols = pl.ds(pl.multiple_of((h * kvl + j) * width, width), width)
        return pltpu.make_async_copy(
            q_ref.at[:, cols], qbufs[j].at[half_own, at_own, :], local_sem.at[2, j]
        )

    def local_base():
        return pltpu.make_async_copy(res_ref, base, base_sem.at[0])

    def local_probe():
        return [
            pltpu.make_async_copy(gain_hbm, gain_ref, base_sem.at[1]),
            pltpu.make_async_copy(weight_hbm, weight_ref, base_sem.at[2]),
        ]

    def cross_kv(j, k):
        to = (h + k) % heads
        cols = pl.ds(pl.multiple_of((to * kvl + j) * HEAD_DIM, HEAD_DIM), HEAD_DIM)
        return [
            pltpu.make_async_remote_copy(
                src_ref=ref.at[:, cols],
                dst_ref=kvbufs[j].at[me, half_own, at_own, pl.ds(i * HEAD_DIM, HEAD_DIM)],
                send_sem=xkv_send.at[i, j, k],
                recv_sem=xkv_recv.at[i, j, k],
                device_id={"head": to},
                device_id_type=MESH,
            )
            for i, ref in enumerate((k_ref, v_ref))
        ]

    def cross_kv_arrived(j, k):
        half, at = rows_of((h + heads - k) % heads)
        for i in range(2):
            piece = kvbufs[j].at[me, half, at, pl.ds(i * HEAD_DIM, HEAD_DIM)]
            pltpu.make_async_copy(piece, piece, xkv_recv.at[i, j, k]).wait()

    def cross_q(j, k):
        to = (h + k) % heads
        cols = pl.ds(pl.multiple_of((to * kvl + j) * width, width), width)
        return pltpu.make_async_remote_copy(
            src_ref=q_ref.at[:, cols],
            dst_ref=qbufs[j].at[half_own, at_own, :],
            send_sem=xq_send.at[j, k],
            recv_sem=xq_recv.at[j, k],
            device_id={"head": to},
            device_id_type=MESH,
        )

    def queries_here(j):
        local_q(j).wait()
        for k in range(1, heads):
            half, at = rows_of((h + heads - k) % heads)
            piece = qbufs[j].at[half, at, :]
            pltpu.make_async_copy(piece, piece, xq_recv.at[j, k]).wait()

    def piece_of(j, s, r, d):
        away = (place + n - s) % n if d == 0 else (place + s) % n
        half, at = rows_of(r)
        return kvbufs[j].at[index_of(away), half, at, :]

    def hop(j, s, r, d):
        piece = piece_of(j, s, r, d)
        return pltpu.make_async_remote_copy(
            src_ref=piece,
            dst_ref=piece,
            send_sem=ring_send.at[j, s, r],
            recv_sem=ring_recv.at[j, s, r],
            device_id={"blk": right if d == 0 else left},
            device_id_type=MESH,
        )

    def hop_arrived(j, s, r, d):
        piece = piece_of(j, s, r, d)
        pltpu.make_async_copy(piece, piece, ring_recv.at[j, s - 1, r]).wait()

    def first_hop(j, r):
        @pl.when(r < per_half)
        def _():
            hop(j, 0, r, 0).start()

        @pl.when(r >= per_half)
        def _():
            hop(j, 0, r, 1).start()

    def first_hops(j):
        for copy in local_kv(j):
            copy.wait()
        first_hop(j, h)
        for k in range(1, heads):
            cross_kv_arrived(j, k)
            first_hop(j, (h + heads - k) % heads)

    def service(j, s):
        for i in range(per_half):
            for d in range(2):
                r = d * per_half + i
                hop_arrived(j, s, r, d)

                @pl.when(s < n - 1)
                def _():
                    hop(j, s, r, d).start()

    for j in range(kvl):
        for k in range(1, heads):
            for copy in cross_kv(j, k):
                copy.start()
    for j in range(kvl):
        for copy in local_kv(j):
            copy.start()
    for j in range(kvl):
        for k in range(1, heads):
            cross_q(j, k).start()
    for j in range(kvl):
        local_q(j).start()

    @pl.when(sec == 0)
    def _():
        local_base().start()

    for copy in local_probe():
        copy.start()

    maxima[...] = jnp.full_like(maxima, LOW)
    squares[...] = jnp.zeros_like(squares)
    products[...] = jnp.zeros_like(products)
    accs[most_lower] = jnp.zeros_like(accs[most_lower])
    ones = jnp.ones((ONES, wide * span), jnp.bfloat16)

    lower = jnp.int32(0)
    for b in range(n):
        lower = jnp.where(me == b, order_ref[b], lower)
    upper_steps = steps - (lower + wide) // wide
    scale = math.log2(math.e) / math.sqrt(HEAD_DIM)
    pairs = max(1, group // 2)
    lanes = group * span // pairs
    heads_in = lanes // span

    def where_is(c):
        first = jnp.minimum(c, 2 * n - 1 - c)
        b = jnp.int32(0)
        for i in range(n):
            b = jnp.where(order_ref[i] == first, i, b)
        return b, jnp.where(c < n, 0, 1)

    def turn(j):
        for half in range(2):
            for g in range(group):
                at = slice(g * HEAD_DIM, (g + 1) * HEAD_DIM)
                turned[half, :, g * span : (g + 1) * span] = qbufs[j][half, :, at].T

    def slot_of(t):
        return jnp.maximum(t - calm, 0)

    def chunk(j, t, masked):
        in_upper = t < upper_steps
        half = jnp.where(in_upper, 1, 0)
        own = jnp.where(in_upper, 2 * n - 1 - lower, lower)
        key = jnp.where(in_upper, upper_steps - 1 - t, t - upper_steps)
        fresh = jnp.logical_or(t == 0, t == upper_steps)
        places = [where_is(wide * key + i) for i in range(wide)]
        blocks = [kvbufs[j][b, which] for b, which in places]
        keys = jnp.concatenate([block[:, :HEAD_DIM] for block in blocks], axis=0)
        values = jnp.concatenate([block[:, HEAD_DIM:].T for block in blocks], axis=1)
        values = jnp.concatenate([values, ones], axis=0)
        if masked:
            limit = (own - wide * key) * span
            ahead = lax.broadcasted_iota(jnp.int32, (wide * span, span), 0) - lax.broadcasted_iota(
                jnp.int32, (wide * span, span), 1
            )
            seen = jnp.concatenate([ahead <= limit] * heads_in, axis=1)
        before = jnp.where(t == 0, most_lower, slot_of(t - 1))
        now = slot_of(t)
        old_max = jnp.where(fresh, LOW, maxima[before])

        def at(p):
            return slice(p * lanes, (p + 1) * lanes)

        def scores_of(p):
            return jnp.dot(keys, turned[half, :, at(p)], preferred_element_type=jnp.float32)

        def soften(p, scores):
            if masked:
                scores = jnp.where(seen, scores, LOW)
            new_max = jnp.maximum(old_max[:, at(p)], jnp.max(scores, axis=0, keepdims=True))
            weights = jnp.exp2(((scores - new_max) * scale).astype(jnp.bfloat16))
            fade = jnp.exp2((old_max[:, at(p)] - new_max) * scale)
            return new_max, fade, jnp.dot(values, weights, preferred_element_type=jnp.float32)

        def keep(p, results):
            new_max, fade, mixed = results
            accs[now, :, at(p)] = accs[before, :, at(p)] * fade + mixed
            maxima[now, :, at(p)] = new_max

        coming = scores_of(0)
        held = None
        for p in range(pairs):
            scores = coming
            if p + 1 < pairs:
                coming = scores_of(p + 1)
            results = soften(p, scores)
            if held is not None:
                keep(p - 1, held)
            held = results
        keep(pairs - 1, held)

    def hand(j):
        piece = base.at[:, pl.ds(pl.multiple_of(j * width, width), width)]
        return pltpu.make_async_remote_copy(
            src_ref=out_ref.at[0, :, pl.ds(pl.multiple_of(j * width, width), width)],
            dst_ref=piece,
            send_sem=hand_send.at[j],
            recv_sem=hand_recv.at[j],
            device_id={"section": 1 - sec},
            device_id_type=MESH,
        )

    def finish(j):
        if j == 0:

            @pl.when(sec == 0)
            def _():
                local_base().wait()

            for copy in local_probe():
                copy.wait()

        @pl.when(sec == 1)
        def _():
            hand(j).wait_recv()

        for half in range(2):
            slot = most_lower if half == 0 else slot_of(upper_steps - 1)
            inverse = 1.0 / accs[slot, HEAD_DIM : HEAD_DIM + 1, :]
            for g in range(group):
                at = slice(g * span, (g + 1) * span)
                cols = pl.ds(pl.multiple_of(j * width + g * HEAD_DIM, HEAD_DIM), HEAD_DIM)
                r = slice(half * span, (half + 1) * span)
                attended = (accs[slot, :HEAD_DIM, at] * inverse[:, at]).T
                stream = (base[r, cols].astype(jnp.float32) + attended).astype(jnp.bfloat16)
                out_ref[0, r, cols] = stream
                wide = stream.astype(jnp.float32)
                squares[half] += wide * wide
                products[half] += wide * (gain_ref[:, cols] * weight_ref[:, cols])

        @pl.when(sec == 0)
        def _():
            hand(j).start()

    stagger = max(1, (n - 1) // 3)
    first_hops(0)

    def slot(time, carry):
        for j in range(kvl):
            s = time - j * stagger

            @pl.when(jnp.logical_and(s >= 1, s < n))
            def _():
                service(j, s)

            if j:

                @pl.when(s == 0)
                def _():
                    first_hops(j)

        return carry

    lax.fori_loop(1, n, slot, 0)
    for j in range(kvl):
        queries_here(j)
        turn(j)
        later = kvl - 1 - j
        apart = max(1, steps // max(1, later * stagger))

        def one(t, carry, j=j, later=later, apart=apart):
            edge = jnp.logical_or(t == 0, t == steps - 1)

            @pl.when(edge)
            def _():
                chunk(j, t, True)

            @pl.when(jnp.logical_not(edge))
            def _():
                chunk(j, t, False)

            for i in range(later):
                turn_of = (t + 1) // apart - 1

                @pl.when(
                    jnp.logical_and((t + 1) % apart == 0, turn_of % later == i)
                )
                def _():
                    s = n + j * stagger + turn_of // later - (j + 1 + i) * stagger

                    @pl.when(jnp.logical_and(s >= 1, turn_of < later * stagger))
                    def _():
                        service(j + 1 + i, s)

                    if i:

                        @pl.when(jnp.logical_and(s == 0, turn_of < later * stagger))
                        def _():
                            first_hops(j + 1 + i)

            return carry

        lax.fori_loop(0, steps, one, 0)
        for i in range(steps // apart, later * stagger):
            s = n + j * stagger + i // later - (j + 1 + i % later) * stagger
            if s >= 1:
                service(j + 1 + i % later, s)
            elif s == 0:
                first_hops(j + 1 + i % later)
        finish(j)

    def totals_of(ref):
        return [jnp.sum(ref[half].T, axis=0, keepdims=True) for half in range(2)]

    parts[h] = jnp.concatenate(totals_of(squares) + totals_of(products), axis=0)

    def share(k):
        return pltpu.make_async_remote_copy(
            src_ref=parts.at[h],
            dst_ref=parts.at[h],
            send_sem=part_send.at[k],
            recv_sem=part_recv.at[k],
            device_id={"head": (h + k) % heads},
            device_id_type=MESH,
        )

    for k in range(1, heads):
        share(k).start()
    for k in range(1, heads):
        piece = parts.at[(h + heads - k) % heads]
        pltpu.make_async_copy(piece, piece, part_recv.at[k]).wait()
    both = parts[0]
    for k in range(1, heads):
        both = both + parts[k]
    features = heads * kvl * width
    reward = both[2:4] * lax.rsqrt(both[0:2] / features + 1e-05)
    reward_ref[...] = jnp.concatenate([reward[:1], reward[1:]], axis=1)

    for k in range(1, heads):
        share(k).wait_send()
        for j in range(kvl):
            for copy in cross_kv(j, k):
                copy.wait_send()
            cross_q(j, k).wait_send()
    for j in range(kvl):

        def sent(s, carry, j=j):
            for r in range(heads):
                hop(j, s, r, r // per_half).wait_send()
            return carry

        lax.fori_loop(0, n - 1, sent, 0)

    @pl.when(sec == 0)
    def _():
        for j in range(kvl):
            hand(j).wait_send()


def body(queries, key_vectors, value_vectors, residual, pair_order, probe_gain, probe_weight):
    n = lax.axis_size("blk")
    heads = lax.axis_size("head")
    rows, features = queries.shape[1:]
    kvl = key_vectors.shape[2] // HEAD_DIM // heads
    group = features // key_vectors.shape[2]
    span = residual.shape[0] // 2
    width = group * HEAD_DIM
    local = residual.shape[1]
    sizes = (n, heads, kvl, group, span, rows)
    dma = pltpu.SemaphoreType.DMA
    hbm = pl.BlockSpec(memory_space=pltpu.HBM)
    vmem = pl.BlockSpec(memory_space=pltpu.VMEM)
    slots = n // 2 + 1
    stream, reward = pl.pallas_call(
        functools.partial(kernel, sizes),
        out_shape=(
            jax.ShapeDtypeStruct((1, 2 * span, local), jnp.bfloat16),
            jax.ShapeDtypeStruct((1, 2 * span), jnp.float32),
        ),
        in_specs=[pl.BlockSpec(memory_space=pltpu.SMEM)] + [hbm] * 6,
        out_specs=(vmem, vmem),
        scratch_shapes=[
            [pltpu.VMEM((n, 2, span, 2 * HEAD_DIM), jnp.bfloat16)] * kvl,
            [pltpu.VMEM((2, span, width), jnp.bfloat16)] * kvl,
            pltpu.VMEM((2, HEAD_DIM, group * span), jnp.bfloat16),
            pltpu.VMEM((2 * span, local), jnp.bfloat16),
            pltpu.VMEM((1, local), jnp.float32),
            pltpu.VMEM((1, local), jnp.float32),
            pltpu.VMEM((slots, HEAD_DIM + ONES, group * span), jnp.float32),
            pltpu.VMEM((slots, 1, group * span), jnp.float32),
            pltpu.VMEM((2, span, HEAD_DIM), jnp.float32),
            pltpu.VMEM((2, span, HEAD_DIM), jnp.float32),
            pltpu.VMEM((heads, 4, span), jnp.float32),
            dma((3, kvl)),
            dma((3,)),
            dma((2, kvl, heads)),
            dma((2, kvl, heads)),
            dma((kvl, heads)),
            dma((kvl, heads)),
            dma((kvl, n, heads)),
            dma((kvl, n, heads)),
            dma((kvl,)),
            dma((kvl,)),
            dma((heads,)),
            dma((heads,)),
        ],
        compiler_params=pltpu.CompilerParams(
            collective_id=0, has_side_effects=True, vmem_limit_bytes=58 * 1024 * 1024
        ),
        name="attention",
    )(pair_order, queries[0], key_vectors[0], value_vectors[0], residual, probe_gain, probe_weight)
    return stream, reward


def solution(mesh):
    return jax.shard_map(
        body,
        mesh=mesh,
        in_specs=(
            P("section", ("blk", "head"), None),
            P("section", ("blk", "head"), None),
            P("section", ("blk", "head"), None),
            P("blk", "head"),
            P(),
            P("section", "head"),
            P("section", "head"),
        ),
        out_specs=(P("section", "blk", "head"), P("section", "blk")),
        check_vma=False,
    )
```
